32 devices in a mesh: slot: 4 (over y, x), seq: 8 (over z, core).
Axes of the slice: x: 2, y: 2, z: 4, core: 2. Of those that a mesh axis runs over, the one named last changes fastest.
Arguments:
- hidden_in: bfloat16 [6144, 2048], P(('slot', 'seq')), may hold values from -6 to 6
- seq_lens: int32 [4, 8], P('slot'), may hold values from 1 to 1216, as said below
- group_order: int32 [4, 16], P('slot'), may hold values from 0 to 15, as said below
- attn_gain: bfloat16 [2048], P(('slot', 'seq')), may hold values from 0.5 to 1.5
- wq_down: bfloat16 [2048, 1024], P(('slot', 'seq')), may hold values from -0.125 to 0.125
- q_gain: bfloat16 [1024], P(('slot', 'seq')), may hold values from 0.5 to 1.5
- wq_up: bfloat16 [1024, 4096], P(('slot', 'seq')), may hold values from -0.1875 to 0.1875
- w_key: bfloat16 [2048, 256], P(('slot', 'seq')), may hold values from -0.125 to 0.125
- w_value: bfloat16 [2048, 256], P(('slot', 'seq')), may hold values from -0.125 to 0.125
- w_out: bfloat16 [4096, 2048], P(('slot', 'seq')), may hold values from -0.375 to 0.375
- ffn_gain: bfloat16 [2048], P(('slot', 'seq')), may hold values from 0.5 to 1.5
- w_gate: bfloat16 [2048, 5632], P(('slot', 'seq')), may hold values from -0.125 to 0.125
- w_up: bfloat16 [2048, 5632], P(('slot', 'seq')), may hold values from -0.125 to 0.125
- w_down: bfloat16 [5632, 2048], P(('slot', 'seq')), may hold values from -0.078125 to 0.078125
- out_grad: bfloat16 [6144, 2048], P(('slot', 'seq')), may hold values from -6 to 6
Outputs:
- layer_out: bfloat16 [6144, 2048], P(('slot', 'seq'))
- in_grad: bfloat16 [6144, 2048], P(('slot', 'seq'))
- grad_attn_gain: float32 [2048], P(('slot', 'seq'))
- grad_wq_down: float32 [2048, 1024], P(('slot', 'seq'))
- grad_q_gain: float32 [1024], P(('slot', 'seq'))
- grad_wq_up: float32 [1024, 4096], P(('slot', 'seq'))
- grad_w_key: float32 [2048, 256], P(('slot', 'seq'))
- grad_w_value: float32 [2048, 256], P(('slot', 'seq'))
- grad_w_out: float32 [4096, 2048], P(('slot', 'seq'))
- grad_ffn_gain: float32 [2048], P(('slot', 'seq'))
- grad_w_gate: float32 [2048, 5632], P(('slot', 'seq'))
- grad_w_up: float32 [2048, 5632], P(('slot', 'seq'))
- grad_w_down: float32 [5632, 2048], P(('slot', 'seq'))
The draws below stay inside these ranges and needn't reach their ends.
Inputs may be any that keep to these rules, and one draw needn't show every extreme that they name: `seq_lens`: sequences lie end to end from slot position 0; the rest of the slot is padding, under 1/16 of 1536 plus 8. The first is at least 1024 long and is the longest; in some slot it is exactly the most. `group_order`: row s lists, for the d-th device along seq, the two blocks of 96 slot positions that it stores, at entries 2 d and 2 d + 1: entry 2 d is d and entry 2 d + 1 lies in the upper half; each block appears once.
All inputs are finite; a program needn't handle non-finite values.
Results may differ from the reference program's by a relative error of at most 0.02.
Values may be sent and summed in bfloat16 or wider, within the bound.
No kernel may reach another device: no remote copies, remote signals or barrier semaphores. Data moves between devices by JAX's collectives and lax.ppermute only.
A program may use at most 384 MiB of HBM per device.

```python
import jax
import jax.numpy as jnp
from jax import lax

D = 2048
H = 16
HD = 256
QR = 1024
FF = 5632
TOK_DEV = 192
NSEQ = 8
SLOTS = 4
SLOT_LEN = 1536
GROUP = 96
GROUPS = 16
TOKENS = 6144


def draw_seq_lens(key, part):
    key = jax.random.fold_in(key, 11)
    lead_key, pad_key, weight_key, pick_key = jax.random.split(key, 4)
    longest = SLOT_LEN * 2 // 3 + SLOT_LEN // 8
    leading = SLOT_LEN * 2 // 3 + jax.random.randint(lead_key, (SLOTS,), 0, SLOT_LEN // 8 + 1)
    chosen = jax.random.randint(pick_key, (), 0, SLOTS)
    leading = jnp.where(jnp.arange(SLOTS, dtype=jnp.int32) == chosen, longest, leading)
    padding = jax.random.randint(pad_key, (SLOTS,), 0, SLOT_LEN // 16 + 1)
    remaining = SLOT_LEN - leading - padding - (NSEQ - 1)
    powers = jax.random.randint(weight_key, (SLOTS, NSEQ - 1), 0, 6)
    weights = jnp.left_shift(jnp.ones_like(powers), powers)
    shares = 1 + weights * remaining[:, None] // jnp.sum(weights, axis=1, keepdims=True)
    return jnp.concatenate([leading[:, None], shares], axis=1).astype(jnp.int32)


def draw_group_order(key, part):
    key = jax.random.fold_in(key, 23)
    later = jax.vmap(lambda subkey: jax.random.permutation(subkey, GROUPS // 2))(jax.random.split(key, SLOTS))
    earlier = jnp.broadcast_to(jnp.arange(GROUPS // 2, dtype=jnp.int32), (SLOTS, GROUPS // 2))
    joined = jnp.stack([earlier, later.astype(jnp.int32) + GROUPS // 2], axis=2)
    return joined.reshape(SLOTS, GROUPS).astype(jnp.int32)


def block_levels(own_key, extent, cuts, low, largest):
    factor_of = 1.0
    for dim, shards_of in cuts:
        draws = jax.random.uniform(jax.random.fold_in(jax.random.fold_in(own_key, 6), dim), (shards_of,), jnp.float32, low / len(cuts), largest / len(cuts))
        factor_of = factor_of * jnp.repeat(jnp.exp(draws), extent[dim] // shards_of).reshape((-1,) + (1,) * (len(extent) - 1 - dim))
    return factor_of


def normal_values(own_key, dims, scale, reach, cuts=(), kind=jnp.bfloat16):
    gain = block_levels(own_key, dims, cuts, -0.22, 0.18) if cuts else 1.0
    values = jax.random.normal(own_key, dims, jnp.float32) * scale * gain
    return jnp.minimum(jnp.maximum(values, -reach), reach).astype(kind)


def setup_inputs(seed: int = 0) -> dict:
    splits = jax.random.split(jax.random.key(seed), 16)
    hidden_in = normal_values(splits[0], (TOKENS, D), 1.0, 6.0, ((0, 32),))
    seq_lens = draw_seq_lens(jax.random.fold_in(splits[15], 71), 0)
    group_order = draw_group_order(jax.random.fold_in(splits[15], 71), 0)
    attn_gain = jnp.clip(1.0 + 0.1 * jax.random.normal(splits[3], (D,), jnp.float32), 0.5, 1.5).astype(jnp.bfloat16)
    wq_down = normal_values(splits[4], (D, QR), D ** -0.5, 0.125, ((0, 32),))
    q_gain = jnp.clip(1.0 + 0.1 * jax.random.normal(splits[5], (QR,), jnp.float32), 0.5, 1.5).astype(jnp.bfloat16)
    wq_up = normal_values(splits[6], (QR, H * HD), QR ** -0.5, 0.1875, ((0, 32),))
    w_key = normal_values(splits[7], (D, HD), D ** -0.5, 0.125, ((0, 32),))
    w_value = normal_values(splits[8], (D, HD), D ** -0.5, 0.125, ((0, 32),))
    w_out = normal_values(splits[9], (H * HD, D), (H * HD // 16) ** -0.5, 0.375, ((0, 32),))
    ffn_gain = jnp.clip(1.0 + 0.1 * jax.random.normal(splits[10], (D,), jnp.float32), 0.5, 1.5).astype(jnp.bfloat16)
    w_gate = normal_values(splits[11], (D, FF), D ** -0.5, 0.125, ((0, 32),))
    w_up = normal_values(splits[12], (D, FF), D ** -0.5, 0.125, ((0, 32),))
    w_down = normal_values(splits[13], (FF, D), FF ** -0.5, 0.078125, ((0, 32),))
    out_grad = normal_values(splits[14], (TOKENS, D), 1.0, 6.0, ((0, 32),))
    return dict(hidden_in=hidden_in, seq_lens=seq_lens, group_order=group_order, attn_gain=attn_gain, wq_down=wq_down, q_gain=q_gain, wq_up=wq_up, w_key=w_key, w_value=w_value, w_out=w_out, ffn_gain=ffn_gain, w_gate=w_gate, w_up=w_up, w_down=w_down, out_grad=out_grad)


@jax.custom_vjp
def low(v):
    return lax.optimization_barrier(v.astype(jnp.bfloat16)).astype(jnp.float32)

@jax.custom_vjp
def low_back(v):
    return v

def low_keep(v):
    return (low(v), None)

def low_pass(kept, grad):
    return (grad,)

def back_keep(v):
    return (v, None)

def back_low(kept, grad):
    return (low(grad),)
low.defvjp(low_keep, low_pass)
low_back.defvjp(back_keep, back_low)
EPS = 1e-05
ROPE_BASE = 10000.0

def norm_scale(values):
    return lax.rsqrt(lax.optimization_barrier(jnp.mean(values * values, axis=-1, keepdims=True)) + EPS)

def rope_tables(position, width):
    half = width // 2
    freq = ROPE_BASE ** (-2.0 * jnp.arange(half, dtype=jnp.float32) / width)
    angle = position.astype(jnp.float32)[:, None] * freq[None, :]
    return (jnp.cos(angle), jnp.sin(angle))

def rotate(values, cosine, sine):
    half = values.shape[-1] // 2
    first = values[..., :half]
    second = values[..., half:]
    return jnp.concatenate([first * cosine - second * sine, first * sine + second * cosine], axis=-1)

def place_info(row_index, order, lengths):
    device = row_index // TOK_DEV
    local = row_index % TOK_DEV
    pick = (2 * device + local // GROUP).astype(jnp.int32)
    table = jnp.arange(order.shape[0], dtype=jnp.int32)
    group_id = lax.optimization_barrier(jnp.sum(jnp.where(pick[:, None] == table[None, :], order[None, :], 0), axis=1)).astype(jnp.int32)
    slot_pos = (group_id * GROUP + local % GROUP).astype(jnp.int32)
    ends = jnp.cumsum(lengths).astype(jnp.int32)
    passed = slot_pos[:, None] >= ends[None, :]
    segment = lax.optimization_barrier(jnp.sum(passed.astype(jnp.int32), axis=1)).astype(jnp.int32)
    start = lax.optimization_barrier(jnp.sum(jnp.where(passed, lengths[None, :], 0), axis=1)).astype(jnp.int32)
    return (slot_pos, segment, (slot_pos - start).astype(jnp.int32), segment < lengths.shape[0])

def product(left, right):
    return jnp.dot(left, right, precision=lax.Precision.HIGHEST)

def slot_attention(pieces):
    query, keys, values, slot_pos, segment = pieces
    allowed = (segment[:, None] == segment[None, :]) & (slot_pos[None, :] <= slot_pos[:, None])

    def one_head(head_query):
        scores = low_back(product(head_query, keys.T))
        masked = jnp.where(allowed, scores, -1e+30)
        top = lax.optimization_barrier(jnp.max(masked, axis=1, keepdims=True))
        weights = jnp.where(allowed, jnp.exp(masked - top), 0.0)
        prob = weights / lax.optimization_barrier(jnp.sum(weights, axis=1, keepdims=True))
        return product(low(prob), values)
    heads = lax.map(jax.checkpoint(one_head), jnp.transpose(query, (1, 0, 2)))
    return jnp.transpose(heads, (1, 0, 2))

def reference(hidden_in, seq_lens, group_order, attn_gain, wq_down, q_gain, wq_up, w_key, w_value, w_out, ffn_gain, w_gate, w_up, w_down, out_grad):
    row_index = jnp.arange(SLOT_LEN, dtype=jnp.int32)
    slot_pos, segment, seq_pos, valid = jax.vmap(lambda order, lengths: place_info(row_index, order, lengths))(group_order, seq_lens)
    cosine, sine = rope_tables(seq_pos.reshape(-1), HD)
    scale = 1.0 / HD ** 0.5

    def forward(inputs, gain_one, down_q, gain_q, up_q, key_proj, value_proj, out_proj, gain_two, gate_proj, up_proj, down_proj):
        normed_one = low(inputs * norm_scale(inputs) * gain_one)
        query_low = low_back(product(normed_one, down_q))
        query_normed = low(query_low * norm_scale(query_low) * gain_q)
        query_full = low_back(product(query_normed, up_q)).reshape(TOKENS, H, HD)
        query_rows = low(rotate(query_full, cosine[:, None, :], sine[:, None, :]) * scale)
        keys_rot = low(rotate(low_back(product(normed_one, key_proj)), cosine, sine))
        values_here = low(low_back(product(normed_one, value_proj)))
        attended = lax.map(jax.checkpoint(slot_attention), (query_rows.reshape(SLOTS, SLOT_LEN, H, HD), keys_rot.reshape(SLOTS, SLOT_LEN, HD), values_here.reshape(SLOTS, SLOT_LEN, HD), slot_pos, segment))
        att_low = low(low_back(attended.reshape(TOKENS, H * HD)))
        middle = inputs + low_back(product(att_low, out_proj))
        normed_two = low(middle * norm_scale(middle) * gain_two)
        gate = low_back(product(normed_two, gate_proj))
        upward = low_back(product(normed_two, up_proj))
        hidden = low(jax.nn.silu(gate) * upward)
        return middle + low_back(product(hidden, down_proj))
    floats = [value.astype(jnp.float32) for value in (hidden_in, attn_gain, wq_down, q_gain, wq_up, w_key, w_value, w_out, ffn_gain, w_gate, w_up, w_down)]
    result, pullback = jax.vjp(forward, *floats)
    cotangent = out_grad.astype(jnp.float32) * valid.reshape(-1)[:, None].astype(jnp.float32)
    grads = pullback(cotangent)
    return (result.astype(jnp.bfloat16), grads[0].astype(jnp.bfloat16), grads[1], grads[2], grads[3], grads[4], grads[5], grads[6], grads[7], grads[8], grads[9], grads[10], grads[11])
```

```python
import functools
import math

import jax
import jax.numpy as jnp
from jax import lax
from jax.sharding import Mesh
from jax.sharding import PartitionSpec as P

H = 16
HD = 256
GROUP = 96

EPS = 1e-05
ROPE_BASE = 10000.0
BF = jnp.bfloat16
F32 = jnp.float32


def norm_scale(values):
    return lax.rsqrt(jnp.mean(values * values, axis=-1, keepdims=True) + EPS)


def norm_back(values, scale, gain, upstream):
    scaled = gain * upstream
    gain_grad = jnp.sum(upstream * values * scale, axis=0)
    inner = jnp.mean(scaled * values, axis=-1, keepdims=True)
    return (gain_grad, scale * scaled - values * scale * scale * scale * inner)


def rope_tables(position, width):
    half = width // 2
    freq = ROPE_BASE ** (-2.0 * jnp.arange(half, dtype=F32) / width)
    angle = position.astype(F32)[:, None] * freq[None, :]
    return (jnp.cos(angle), jnp.sin(angle))


def rotate(values, cosine, sine):
    half = values.shape[-1] // 2
    first = values[..., :half]
    second = values[..., half:]
    return jnp.concatenate(
        [first * cosine - second * sine, first * sine + second * cosine], axis=-1
    )


def unrotate(grads, cosine, sine):
    half = grads.shape[-1] // 2
    first = grads[..., :half]
    second = grads[..., half:]
    return jnp.concatenate(
        [first * cosine + second * sine, second * cosine - first * sine], axis=-1
    )


def place_info(row_index, order, lengths, tokens):
    device = row_index // tokens
    local = row_index % tokens
    pick = 2 * device + local // GROUP
    table = jnp.arange(order.shape[0], dtype=jnp.int32)
    group_id = jnp.sum(jnp.where(pick[:, None] == table[None, :], order[None, :], 0), axis=1)
    slot_pos = group_id * GROUP + local % GROUP
    ends = jnp.cumsum(lengths)
    passed = slot_pos[:, None] >= ends[None, :]
    segment = jnp.sum(passed.astype(jnp.int32), axis=1)
    start = jnp.sum(jnp.where(passed, lengths[None, :], 0), axis=1)
    return (slot_pos, segment, slot_pos - start, segment < lengths.shape[0])


def block_size(count):
    size = min(512, count)
    while count % size:
        size -= 1
    return size


def dot(left, right):
    return jnp.dot(left, right, preferred_element_type=F32)


def contract_last(left, right):
    return lax.dot_general(left, right, (((1,), (1,)), ((), ())), preferred_element_type=F32)


def contract_first(left, right):
    return lax.dot_general(left, right, (((0,), (0,)), ((), ())), preferred_element_type=F32)


class Net:
    def __init__(self, slots, depth):
        self.S = slots
        self.Z = depth

    def slot(self):
        return lax.axis_index("slot")

    def core(self):
        return lax.axis_index("c")

    def swap_c(self, a):
        return lax.ppermute(a, "c", [(0, 1), (1, 0)])

    def swap_x(self, a):
        return lax.ppermute(a, "slot", [(0, 1), (1, 0), (2, 3), (3, 2)])

    def swap_y(self, a):
        return lax.ppermute(a, "slot", [(0, 2), (2, 0), (1, 3), (3, 1)])

    def relative(self, number):
        return self.slot() ^ number if self.S == 4 else number

    def slots_gather(self, a):
        if self.S != 4:
            return lax.all_gather(a, "slot", axis=0, tiled=True)
        half = a.shape[0] // 2
        ax = self.swap_x(a)
        ay = self.swap_y(a)
        d0 = self.swap_y(ax[:half])
        d1 = self.swap_x(ay[half:])
        return jnp.concatenate([a, ax, ay, d0, d1], axis=0)

    def plane_gather(self, a):
        same = self.slots_gather(a)
        return same, self.swap_c(same)

    def plane_scatter(self, same, other):
        held = same.astype(F32) + self.swap_c(other).astype(F32)
        if self.S != 4:
            return lax.psum_scatter(
                held.astype(BF), "slot", scatter_dimension=0, tiled=True
            ).astype(F32)
        n = same.shape[0] // 4
        half = n // 2
        parts = held.reshape(4, n, -1)
        left = parts[:, :half]
        right = parts[:, half:]
        via_x = self.swap_x(jnp.concatenate([left[1], left[3]], axis=0).astype(BF)).astype(F32)
        via_y = self.swap_y(jnp.concatenate([right[2], right[3]], axis=0).astype(BF)).astype(F32)
        left_own = left[0] + via_x[:half]
        right_own = right[0] + via_y[: n - half]
        left_last = self.swap_y((left[2] + via_x[half:]).astype(BF)).astype(F32)
        right_last = self.swap_x((right[1] + via_y[n - half :]).astype(BF)).astype(F32)
        return jnp.concatenate([left_own + left_last, right_own + right_last], axis=0)

    def gather_all(self, w):
        r, n = w.shape
        same, other = self.plane_gather(lax.all_gather(w, "z", axis=0, tiled=True))
        first = self.core() == 0
        same = same.reshape(self.S, self.Z, 1, r, n)
        other = other.reshape(self.S, self.Z, 1, r, n)
        rows = []
        for number in range(self.S):
            place = self.relative(number)
            mine = lax.dynamic_slice_in_dim(same, place, 1, 0)
            theirs = lax.dynamic_slice_in_dim(other, place, 1, 0)
            rows.append(
                jnp.concatenate(
                    [jnp.where(first, mine, theirs), jnp.where(first, theirs, mine)], axis=2
                )
            )
        return jnp.concatenate(rows, axis=0).reshape(self.S * self.Z * 2 * r, n)

    def scatter_all(self, g):
        n = g.shape[1]
        r = g.shape[0] // (self.S * self.Z * 2)
        parts = g.astype(BF).reshape(self.S, self.Z, 2, r, n)

        def side(core):
            picked = lax.dynamic_slice_in_dim(parts, core, 1, 2)
            return jnp.concatenate(
                [
                    lax.dynamic_slice_in_dim(picked, self.relative(number), 1, 0)
                    for number in range(self.S)
                ],
                axis=0,
            ).reshape(self.S * self.Z * r, n)

        summed = self.plane_scatter(side(self.core()), side(1 - self.core()))
        return lax.psum_scatter(summed.astype(BF), "z", scatter_dimension=0, tiled=True).astype(F32)

    def rows_chunk(self, w):
        whole = lax.all_gather(w, ("z", "c"), axis=0, tiled=True)
        size = whole.shape[0] // 2
        return lax.dynamic_slice_in_dim(whole, self.core() * size, size, 0)

    def rows_scatter(self, g):
        n = g.shape[1]
        r = g.shape[0] // self.Z
        parts = g.astype(BF).reshape(self.Z // 2, 2, r, n)
        mine = lax.dynamic_slice_in_dim(parts, self.core(), 1, 1).reshape(-1, n)
        sent = lax.dynamic_slice_in_dim(parts, 1 - self.core(), 1, 1).reshape(-1, n)
        came = self.swap_c(sent)
        first = self.core() == 0
        joined = jnp.concatenate(
            [jnp.where(first, mine, came), jnp.where(first, came, mine)], axis=0
        )
        return lax.psum_scatter(joined, "z", scatter_dimension=0, tiled=True).astype(F32)

    def cols_chunk(self, w):
        r, n = w.shape
        ways = 2 * self.S
        parts = w.reshape(r, ways, n // ways).transpose(1, 0, 2)
        parts = lax.all_to_all(parts, ("slot", "c"), 0, 0, tiled=True)
        return lax.all_gather(parts.reshape(ways * r, n // ways), "z", axis=0, tiled=True)

    def cols_scatter(self, g):
        ways = 2 * self.S
        m = g.shape[1]
        r = g.shape[0] // (self.Z * ways)
        mine = lax.psum_scatter(g.astype(BF), "z", scatter_dimension=0, tiled=True)
        parts = lax.all_to_all(mine.reshape(ways, r, m), ("slot", "c"), 0, 0, tiled=True)
        return parts.transpose(1, 0, 2).reshape(r, ways * m).astype(F32)

    def by_z(self, a):
        t, n = a.shape
        piece = n // (self.S * self.Z)
        parts = [
            a[:, (s * self.Z + z) * piece : (s * self.Z + z + 1) * piece]
            for z in range(self.Z)
            for s in range(self.S)
        ]
        return jnp.concatenate(parts, axis=1)

    def from_z(self, a):
        t, n = a.shape
        piece = n // (self.S * self.Z)
        parts = [
            a[:, (z * self.S + s) * piece : (z * self.S + s + 1) * piece]
            for s in range(self.S)
            for z in range(self.Z)
        ]
        return jnp.concatenate(parts, axis=1)


def attend(query_rows, key_rows, value_rows, query_seg, query_pos, order, lengths, tokens):
    query_count = query_rows.shape[0]
    empty = (
        jnp.full((query_count,), -1e30, F32),
        jnp.zeros((query_count,), F32),
        jnp.zeros((query_count, HD), F32),
    )
    count = key_rows.shape[0]
    size = block_size(count)

    def one_block(state, number):
        top, total, summed = state
        offset = number * size
        key_block = lax.dynamic_slice_in_dim(key_rows, offset, size, 0)
        value_block = lax.dynamic_slice_in_dim(value_rows, offset, size, 0)
        key_index = offset + jnp.arange(size, dtype=jnp.int32)
        key_pos, key_seg, _, _ = place_info(key_index, order, lengths, tokens)
        allowed = (query_seg[:, None] == key_seg[None, :]) & (
            key_pos[None, :] <= query_pos[:, None]
        )
        scores = jnp.where(allowed, contract_last(query_rows, key_block), -1e30)
        new_top = jnp.maximum(top, jnp.max(scores, axis=1))
        fade = jnp.exp(top - new_top)
        weights = jnp.where(allowed, jnp.exp(scores - new_top[:, None]), 0.0)
        total = total * fade + jnp.sum(weights, axis=1)
        summed = summed * fade[:, None] + dot(weights.astype(BF), value_block)
        return ((new_top, total, summed), None)

    state, _ = lax.scan(one_block, empty, jnp.arange(count // size))
    top, total, summed = state
    return summed / total[:, None], top + jnp.log(total)


def attend_back(
    query_rows, keys_all, values_all, att_grad, attended, log_total,
    query_seg, query_pos, order, lengths, tokens,
):
    delta = jnp.sum(att_grad.astype(F32) * attended, axis=1)
    slot_rows = keys_all.shape[0]
    size = block_size(slot_rows)

    def back_block(query_grad, number):
        offset = number * size
        key_block = lax.dynamic_slice_in_dim(keys_all, offset, size, 0)
        value_block = lax.dynamic_slice_in_dim(values_all, offset, size, 0)
        key_index = offset + jnp.arange(size, dtype=jnp.int32)
        key_pos, key_seg, _, _ = place_info(key_index, order, lengths, tokens)
        allowed = (query_seg[:, None] == key_seg[None, :]) & (
            key_pos[None, :] <= query_pos[:, None]
        )
        prob = jnp.where(
            allowed, jnp.exp(contract_last(query_rows, key_block) - log_total[:, None]), 0.0
        )
        prob_grad = contract_last(att_grad, value_block)
        score_grad = (prob * (prob_grad - delta[:, None])).astype(BF)
        value_grad = contract_first(prob.astype(BF), att_grad)
        key_grad = contract_first(score_grad, query_rows)
        query_grad = query_grad + dot(score_grad, key_block)
        return (query_grad, (key_grad, value_grad))

    query_grad, (key_grads, value_grads) = lax.scan(
        back_block, jnp.zeros(query_rows.shape, F32), jnp.arange(slot_rows // size)
    )
    return query_grad, key_grads.reshape(slot_rows, HD), value_grads.reshape(slot_rows, HD)


def column(a, rows):
    return jnp.pad(a.reshape(-1, 1), ((0, rows - a.shape[0]), (0, 0)))


def body(
    net,
    hidden_in, seq_lens, group_order, attn_gain, wq_down, q_gain, wq_up, w_key, w_value, w_out,
    ffn_gain, w_gate, w_up, w_down, out_grad,
):
    lengths = seq_lens[0]
    order = group_order[0]
    tokens = hidden_in.shape[0]
    width = hidden_in.shape[1]
    low_rank = wq_up.shape[0] * net.S * net.Z * 2
    query_count = tokens * H
    scale = 1.0 / math.sqrt(HD)
    place = lax.axis_index("z") * 2 + lax.axis_index("c")
    rows_here = place * tokens + jnp.arange(tokens, dtype=jnp.int32)
    slot_pos, segment, seq_pos, valid = place_info(rows_here, order, lengths, tokens)
    cosine, sine = rope_tables(seq_pos, HD)
    query_seg = jnp.repeat(segment, H)
    query_pos = jnp.repeat(slot_pos, H)

    rows = wq_down.shape[0]
    gains = jnp.concatenate(
        [column(attn_gain, rows), column(ffn_gain, rows), column(q_gain, rows)], axis=1
    )
    gains = jnp.pad(gains, ((0, 0), (0, 128 - 3)))
    first_set = net.gather_all(jnp.concatenate([wq_down, w_key, w_value, gains], axis=1))
    down_q = first_set[:, :low_rank]
    key_proj = first_set[:, low_rank : low_rank + HD]
    value_proj = first_set[:, low_rank + HD : low_rank + 2 * HD]
    gains = first_set[:, low_rank + 2 * HD :].astype(F32)
    gain_one = gains[:, 0]
    gain_two = gains[:, 1]
    gain_q = gains[:, 2].reshape(-1, rows)[:, : q_gain.shape[0]].reshape(-1)
    up_q = net.gather_all(wq_up)
    out_chunk = net.rows_chunk(w_out)
    gate_chunk = net.cols_chunk(w_gate)
    up_chunk = net.cols_chunk(w_up)
    down_chunk = net.rows_chunk(w_down)

    out_cot = out_grad.astype(F32) * valid[:, None].astype(F32)
    cot_sides = net.plane_gather(out_cot.astype(BF))

    inputs = hidden_in.astype(F32)
    scale_one = norm_scale(inputs)
    normed_one = (inputs * scale_one * gain_one).astype(BF)
    query_low = dot(normed_one, down_q)
    scale_q = norm_scale(query_low)
    query_normed = (query_low * scale_q * gain_q).astype(BF)
    query_full = dot(query_normed, up_q).reshape(tokens, H, HD)
    query_rows = (
        (rotate(query_full, cosine[:, None, :], sine[:, None, :]) * scale)
        .astype(BF)
        .reshape(query_count, HD)
    )
    keys_rot = rotate(dot(normed_one, key_proj), cosine, sine).astype(BF)
    values_here = dot(normed_one, value_proj).astype(BF)
    both = lax.all_gather(
        jnp.concatenate([keys_rot, values_here], axis=1), ("z", "c"), axis=0, tiled=True
    )
    key_rows = both[:, :HD]
    value_rows = both[:, HD:]
    attended, log_total = attend(
        query_rows, key_rows, value_rows, query_seg, query_pos, order, lengths, tokens
    )
    ways = 2 * net.S
    att_low = attended.reshape(tokens, ways, H * HD // ways).astype(BF)

    def to_heads(a):
        got = lax.all_to_all(a.transpose(1, 0, 2), ("slot", "c"), 0, 0, tiled=True)
        got = got.reshape(net.S, 2, tokens, -1)

        def side(core):
            picked = lax.dynamic_slice_in_dim(got, core, 1, 1)
            return jnp.concatenate(
                [
                    lax.dynamic_slice_in_dim(picked, net.relative(number), 1, 0)
                    for number in range(net.S)
                ],
                axis=0,
            ).reshape(net.S * tokens, -1)

        return side(net.core()), side(1 - net.core())

    def to_rows(same, other):
        same = same.reshape(net.S, 1, tokens, -1)
        other = other.reshape(net.S, 1, tokens, -1)
        first = net.core() == 0
        pair = jnp.concatenate(
            [jnp.where(first, same, other), jnp.where(first, other, same)], axis=1
        )
        pair = jnp.concatenate(
            [
                lax.dynamic_slice_in_dim(pair, net.relative(number), 1, 0)
                for number in range(net.S)
            ],
            axis=0,
        ).reshape(ways, tokens, -1)
        return lax.all_to_all(pair, ("slot", "c"), 0, 0, tiled=True)

    att_sides = to_heads(att_low)
    mid_part = net.plane_scatter(*[dot(a, out_chunk).astype(BF) for a in att_sides])
    middle = inputs + mid_part

    scale_two = norm_scale(middle)
    normed_two = (middle * scale_two * gain_two).astype(BF)
    normed_sides = net.plane_gather(net.by_z(normed_two))
    gate = [dot(a, gate_chunk) for a in normed_sides]
    upward = [dot(a, up_chunk) for a in normed_sides]
    sigma = [jax.nn.sigmoid(g) for g in gate]
    hidden = [(g * s * u).astype(BF) for g, s, u in zip(gate, sigma, upward)]

    hidden_grad = [contract_last(a, down_chunk) for a in cot_sides]
    gate_grad = [
        (d * u * s * (1.0 + g * (1.0 - s))).astype(BF)
        for d, u, s, g in zip(hidden_grad, upward, sigma, gate)
    ]
    upward_grad = [
        (d * g * s).astype(BF) for d, g, s in zip(hidden_grad, gate, sigma)
    ]
    normed_two_grad = net.from_z(
        net.plane_scatter(
            *[
                (contract_last(a, gate_chunk) + contract_last(b, up_chunk)).astype(BF)
                for a, b in zip(gate_grad, upward_grad)
            ]
        )
    )
    result = middle + net.plane_scatter(*[dot(a, down_chunk).astype(BF) for a in hidden])
    layer_out = result.astype(BF)
    grad_down = sum(contract_first(a, b) for a, b in zip(hidden, cot_sides))
    grad_gate = sum(contract_first(a, b) for a, b in zip(normed_sides, gate_grad))
    grad_upward = sum(contract_first(a, b) for a, b in zip(normed_sides, upward_grad))
    grad_down = net.rows_scatter(grad_down)
    grad_gate = net.cols_scatter(grad_gate)
    grad_upward = net.cols_scatter(grad_upward)
    grad_gain_two, middle_back = norm_back(middle, scale_two, gain_two, normed_two_grad)
    middle_grad = out_cot + middle_back

    middle_sides = net.plane_gather(middle_grad.astype(BF))
    grad_out = sum(contract_first(a, b) for a, b in zip(att_sides, middle_sides))
    grad_out = net.rows_scatter(grad_out)
    att_grad = to_rows(*[contract_last(a, out_chunk).astype(BF) for a in middle_sides])
    att_grad = att_grad.transpose(1, 0, 2).reshape(query_count, HD)
    query_grad, key_grads, value_grads = attend_back(
        query_rows, key_rows, value_rows, att_grad, attended, log_total,
        query_seg, query_pos, order, lengths, tokens,
    )
    both_sum = lax.psum_scatter(
        jnp.concatenate([key_grads, value_grads], axis=1).astype(BF),
        ("z", "c"), scatter_dimension=0, tiled=True,
    ).astype(F32)
    key_pre = unrotate(both_sum[:, :HD], cosine, sine).astype(BF)
    value_pre = both_sum[:, HD:].astype(BF)
    query_pre = (
        unrotate(
            query_grad.reshape(tokens, H, HD) * scale, cosine[:, None, :], sine[:, None, :]
        )
        .reshape(tokens, H * HD)
        .astype(BF)
    )
    grad_up_q = net.scatter_all(contract_first(query_normed, query_pre))
    normed_q_grad = contract_last(query_pre, up_q)
    grad_gain_q, low_part = norm_back(query_low, scale_q, gain_q, normed_q_grad)
    query_low_grad = low_part.astype(BF)
    first_grad = jnp.concatenate([query_low_grad, key_pre, value_pre], axis=1)
    normed_one_grad = contract_last(first_grad, first_set[:, : low_rank + 2 * HD])
    grad_gain_one, input_part = norm_back(inputs, scale_one, gain_one, normed_one_grad)
    in_grad = (middle_grad + input_part).astype(BF)
    q_column = jnp.pad(
        grad_gain_q.reshape(-1, q_gain.shape[0]), ((0, 0), (0, rows - q_gain.shape[0]))
    ).reshape(-1)
    gain_grads = jnp.stack([grad_gain_one, grad_gain_two, q_column], axis=1)
    first_out = net.scatter_all(
        jnp.concatenate(
            [
                contract_first(normed_one, first_grad),
                jnp.pad(gain_grads, ((0, 0), (0, 128 - 3))),
            ],
            axis=1,
        )
    )
    last = low_rank + 2 * HD
    return (
        layer_out,
        in_grad,
        first_out[:, last],
        first_out[:, :low_rank],
        first_out[: q_gain.shape[0], last + 2],
        grad_up_q,
        first_out[:, low_rank : low_rank + HD],
        first_out[:, low_rank + HD : last],
        grad_out,
        first_out[:, last + 1],
        grad_gate,
        grad_upward,
        grad_down,
    )


def solution(mesh):
    slots, seq = mesh.devices.shape
    fine = Mesh(mesh.devices.reshape(slots, seq // 2, 2), ("slot", "z", "c"))
    every = ("slot", "z", "c")
    matrix = P(every, None)
    vector = P(every)
    net = Net(slots, seq // 2)
    return jax.shard_map(
        functools.partial(body, net),
        mesh=fine,
        in_specs=(
            matrix, P("slot", None), P("slot", None), vector, matrix, vector, matrix, matrix,
            matrix, matrix, vector, matrix, matrix, matrix, matrix,
        ),
        out_specs=(
            matrix, matrix, vector, matrix, vector, matrix, matrix, matrix, matrix, vector,
            matrix, matrix, matrix,
        ),
        check_vma=False,
    )
```

```python
import functools
import math

import jax
import jax.numpy as jnp
from jax import lax
from jax.experimental import pallas as pl
from jax.experimental.pallas import tpu as pltpu
from jax.sharding import Mesh
from jax.sharding import PartitionSpec as P

H = 16
HD = 256
GROUP = 96
TILE = 256
HG = 8
VMEM_BYTES = 60 << 20

EPS = 1e-05
ROPE_BASE = 10000.0
BF = jnp.bfloat16
F32 = jnp.float32


class Net:
    def __init__(self, slots, depth):
        self.S = slots
        self.Z = depth

    def me(self):
        return jnp.stack([lax.axis_index("slot"), lax.axis_index("c")]).astype(jnp.int32)

    def whole_pieces(self, rows):
        return self.S != 4

    def segments(self, n):
        if self.S != 4:
            return [(0, 0, n)]
        half = n // 2
        return [(0, 0, n), (1, 0, n), (2, 0, n), (3, 0, half), (3, half, n - half)]

    def swap_c(self, a):
        return lax.ppermute(a, "c", [(0, 1), (1, 0)])

    def swap_x(self, a):
        return lax.ppermute(a, "slot", [(0, 1), (1, 0), (2, 3), (3, 2)])

    def swap_y(self, a):
        return lax.ppermute(a, "slot", [(0, 2), (2, 0), (1, 3), (3, 1)])

    def spread(self, a, during=()):
        first, second = [*during, None, None][:2]
        if self.S != 4:
            a = lax.all_gather(a, "slot", axis=0, tiled=True)
            for step in (first, second):
                if step is not None:
                    (a,) = step(a)
            return [a]
        half = a.shape[0] // 2
        ax = self.swap_x(a)
        ay = self.swap_y(a)
        if first is not None:
            ax, ay = first(ax, ay)
        d0 = self.swap_y(ax[:half])
        d1 = self.swap_x(ay[half:])
        if second is not None:
            d0, d1 = second(d0, d1)
        return [a, ax, ay, d0, d1]

    def swap_all(self, pieces):
        return [self.swap_c(a) for a in pieces]

    def weight_pieces(self, same):
        other = self.swap_all(same)
        if self.S == 4:
            return [*same, *other]
        n = same[0].shape[1]
        r = same[0].shape[0] // (self.S * self.Z)
        first = lax.axis_index("c") == 0
        same = same[0].reshape(self.S, self.Z, 1, r, n)
        other = other[0].reshape(self.S, self.Z, 1, r, n)
        pair = [jnp.where(first, same, other), jnp.where(first, other, same)]
        return [jnp.concatenate(pair, axis=2).reshape(-1, n)]

    def weight_sides(self, parts):
        if self.S == 4:
            return parts[:4], parts[4:]
        n = parts[0].shape[1]
        whole = parts[0].reshape(self.S, self.Z, 2, -1, n)
        r = whole.shape[3]
        core = lax.axis_index("c")
        return tuple(
            [
                lax.dynamic_slice_in_dim(whole[slot], k, 1, 1).reshape(self.Z * r, n)
                for slot in range(self.S)
            ]
            for k in (core, 1 - core)
        )

    def collect(self, same, other, during=()):
        first, second, third = [*during, None, None, None][:3]
        came = self.swap_all(other)
        if first is not None:
            came = first(*came)
        held = [a.astype(F32) + b.astype(F32) for a, b in zip(same, came)]
        half = same[0].shape[0] // 2
        if self.S != 4:
            total = jnp.concatenate(held, axis=0).astype(BF)
            for step in (second, third):
                if step is not None:
                    (total,) = step(total)
            total = lax.psum_scatter(total, "slot", scatter_dimension=0, tiled=True)
            upper, lower = total[:half].astype(F32), total[half:].astype(F32)
            return [upper, jnp.zeros_like(total[:half]), lower, jnp.zeros_like(total[half:])]
        via_x = self.swap_x(jnp.concatenate([held[1][:half], held[3][:half]], axis=0).astype(BF))
        via_y = self.swap_y(jnp.concatenate([held[2][half:], held[3][half:]], axis=0).astype(BF))
        if second is not None:
            via_x, via_y = second(via_x, via_y)
        via_x, via_y = via_x.astype(F32), via_y.astype(F32)
        upper = held[0][:half] + via_x[:half]
        lower = held[0][half:] + via_y[: via_y.shape[0] // 2]
        upper_last = self.swap_y((held[2][:half] + via_x[half:]).astype(BF))
        lower_last = self.swap_x((held[1][half:] + via_y[via_y.shape[0] // 2 :]).astype(BF))
        if third is not None:
            upper_last, lower_last = third(upper_last, lower_last)
        return [upper, upper_last, lower, lower_last]

    def z_gather(self, w):
        return lax.all_gather(w, "z", axis=0, tiled=True)

    def z_scatter(self, g):
        return lax.psum_scatter(g.astype(BF), "z", scatter_dimension=0, tiled=True)

    def rows_gather(self, w):
        return lax.all_gather(w, ("z", "c"), axis=0, tiled=True)

    def rows_return(self, g):
        n = g.shape[1]
        r = g.shape[0] // self.Z
        core = lax.axis_index("c")
        parts = g.reshape(self.Z // 2, 2, r, n)
        mine = lax.dynamic_slice_in_dim(parts, core, 1, 1).reshape(-1, n)
        sent = lax.dynamic_slice_in_dim(parts, 1 - core, 1, 1).reshape(-1, n)
        came = self.swap_c(sent)
        first = core == 0
        return jnp.concatenate(
            [jnp.where(first, mine, came), jnp.where(first, came, mine)], axis=0
        )

    def cols_exchange(self, gate, up):
        r, n = gate.shape
        ways = 2 * self.S
        parts = jnp.concatenate(
            [gate.reshape(r, ways, n // ways), up.reshape(r, ways, n // ways)], axis=2
        ).transpose(1, 0, 2)
        return self.exchange(parts).reshape(ways * r, 2 * n // ways)

    def cols_return(self, mine):
        ways = 2 * self.S
        m = mine.shape[1] // 2
        parts = self.exchange(mine.reshape(ways, -1, 2 * m)).transpose(1, 0, 2)
        r = parts.shape[0]
        return (
            parts[:, :, :m].reshape(r, ways * m).astype(F32),
            parts[:, :, m:].reshape(r, ways * m).astype(F32),
        )

    def exchange(self, a):
        return lax.all_to_all(a, ("slot", "c"), 0, 0, tiled=True)


def tie(*arrays):
    return lax.optimization_barrier(arrays)


def column(a):
    return jnp.pad(a.reshape(-1, 1), ((0, 0), (0, 127)))


def place_info(row_index, order, lengths, tokens):
    device = row_index // tokens
    local = row_index % tokens
    pick = 2 * device + local // GROUP
    table = jnp.arange(order.shape[0], dtype=jnp.int32)
    group_id = jnp.sum(jnp.where(pick[:, None] == table[None, :], order[None, :], 0), axis=1)
    slot_pos = group_id * GROUP + local % GROUP
    ends = jnp.cumsum(lengths)
    passed = slot_pos[:, None] >= ends[None, :]
    segment = jnp.sum(passed.astype(jnp.int32), axis=1)
    start = jnp.sum(jnp.where(passed, lengths[None, :], 0), axis=1)
    return (slot_pos - start, segment < lengths.shape[0])


def rope_tables(position, width):
    half = width // 2
    freq = ROPE_BASE ** (-2.0 * jnp.arange(half, dtype=F32) / width)
    angle = position.astype(F32)[:, None] * freq[None, :]
    return (jnp.cos(angle), jnp.sin(angle))


def contract_first(left, right):
    return lax.dot_general(left, right, (((0,), (0,)), ((), ())), preferred_element_type=F32)


def _call(kernel, name, out_shape, args, scratch=(), memory=None):
    specs = [
        pl.BlockSpec(
            memory_space=pltpu.SMEM
            if a.dtype == jnp.int32 and a.ndim == 1
            else (memory or pltpu.VMEM)
        )
        for a in args
    ]
    many = isinstance(out_shape, (tuple, list))
    out_specs = [pl.BlockSpec(memory_space=memory or pltpu.VMEM)] * (len(out_shape) if many else 1)
    return pl.pallas_call(
        kernel,
        out_shape=out_shape,
        in_specs=specs,
        out_specs=out_specs if many else out_specs[0],
        scratch_shapes=list(scratch),
        compiler_params=pltpu.CompilerParams(vmem_limit_bytes=VMEM_BYTES),
        cost_estimate=pl.CostEstimate(flops=1, bytes_accessed=1, transcendentals=0),
        name=name,
    )(*args)


def _shape(*dims, dtype=BF):
    return jax.ShapeDtypeStruct(dims, dtype)


def _nt(a, b):
    return lax.dot_general(a, b, (((1,), (1,)), ((), ())), preferred_element_type=F32)


def _tn(a, b):
    return lax.dot_general(a, b, (((0,), (0,)), ((), ())), preferred_element_type=F32)


def _row_place(net, me, place, z, other, r):
    slot = jnp.bitwise_xor(me[0], place) if net.S == 4 else place
    core = 1 - me[1] if other else me[1]
    return pl.multiple_of(((slot * net.Z + z) * 2 + core) * r, r)


def _join(net, me, pieces, whole):
    if len(pieces) == 1:
        whole[...] = pieces[0][...]
        return
    r = whole.shape[0] // (net.S * net.Z * 2)
    for side in range(2):
        for (place, first, count), ref in zip(net.segments(net.Z * r), pieces[side * 5 : side * 5 + 5]):
            for k in range(count // r):
                at = _row_place(net, me, place, first // r + k, side == 1, r)
                whole[pl.ds(at, r), :] = ref[k * r : (k + 1) * r, :]


def _part(net, me, whole, pieces):
    if len(pieces) == 1:
        pieces[0][...] = whole[...]
        return
    r = whole.shape[0] // (net.S * net.Z * 2)
    for side in range(2):
        for place in range(net.S):
            for z in range(net.Z):
                at = _row_place(net, me, place, z, side == 1, r)
                pieces[side * net.S + place][z * r : (z + 1) * r, :] = whole[pl.ds(at, r), :]


def _mean_scale(values):
    return lax.rsqrt(jnp.mean(values * values, axis=1, keepdims=True) + EPS)


def project_kernel(net, count, me, x_ref, cos, sin, *refs):
    pieces, (low_out, kv_out, gain_out, whole) = refs[:count], refs[count:]
    _join(net, me, pieces, whole)
    width = whole.shape[0]
    low_rank = low_out.shape[1]
    last = low_rank + 2 * HD
    gains = jnp.transpose(whole[:, last:].astype(F32))
    gain_out[...] = gains[: gain_out.shape[0], :]
    x = x_ref[...].astype(F32)
    normed = (x * _mean_scale(x) * gains[:1, :]).astype(BF)
    low_out[...] = jnp.dot(normed, whole[:, :low_rank], preferred_element_type=F32)
    both = jnp.dot(normed, whole[:, low_rank:last], preferred_element_type=F32)
    half = HD // 2
    a, b = both[:, :half], both[:, half:HD]
    kv_out[:, :half] = (a * cos[...] - b * sin[...]).astype(BF)
    kv_out[:, half:HD] = (a * sin[...] + b * cos[...]).astype(BF)
    kv_out[:, HD:] = both[:, HD:].astype(BF)


def project(net, me, x, cos, sin, pieces, low_rank):
    tokens, width = x.shape
    wide = pieces[0].shape[1]
    return _call(
        functools.partial(project_kernel, net, len(pieces)),
        "project",
        (_shape(tokens, low_rank, dtype=F32), _shape(tokens, 2 * HD), _shape(8, width, dtype=F32)),
        [me, x, cos, sin, *pieces],
        [pltpu.VMEM((width, wide), BF)],
    )


def _starts(pos, table):
    start = jnp.zeros_like(pos)
    count = table.shape[0] // 2
    for k in range(count):
        start = start + jnp.where(pos >= table[k], table[count + k], 0)
    return start


def _start_of(pos, table):
    start = jnp.int32(0)
    count = table.shape[0] // 2
    for k in range(count):
        start = start + jnp.where(pos >= table[k], table[count + k], 0)
    return start


def _span(group, table):
    return _start_of(group * GROUP, table) // TILE, (group * GROUP + GROUP - 1) // TILE + 1


def _stack(ref, rows, first, heads):
    return jnp.concatenate(
        [ref[rows, (first + h) * HD : (first + h + 1) * HD] for h in range(heads)], axis=0
    )


def _sort_keys(order, kv, sorted_kv):
    for b in range(kv.shape[0] // GROUP):
        at = pl.ds(pl.multiple_of(order[b] * GROUP, GROUP), GROUP)
        sorted_kv[at, :] = kv[b * GROUP : (b + 1) * GROUP, :]


def attend_kernel(net, count, table, order, here, me, low, cos, sin, kv, *refs):
    pieces = refs[:count]
    cqn_out, q_out, att_out, chunk_out, lse_out, up_q, sorted_kv, scores = refs[count:]
    _join(net, me, pieces, up_q)
    _sort_keys(order, kv, sorted_kv)
    wide = H * HD
    gain = jnp.transpose(up_q[:, wide:].astype(F32))[:1, :]
    cqn_out[...] = (low[...] * _mean_scale(low[...]) * gain).astype(BF)
    scale = 1.0 / math.sqrt(HD)
    half = HD // 2
    per_chunk = chunk_out.shape[2] // HD
    for h in range(H):
        full = jnp.dot(
            cqn_out[...], up_q[:, h * HD : (h + 1) * HD], preferred_element_type=F32
        )
        a, b = full[:, :half], full[:, half:]
        q_out[:, h * HD : h * HD + half] = ((a * cos[...] - b * sin[...]) * scale).astype(BF)
        q_out[:, h * HD + half : (h + 1) * HD] = (
            (a * sin[...] + b * cos[...]) * scale
        ).astype(BF)
    for blk in range(2):
        rows = slice(blk * GROUP, (blk + 1) * GROUP)
        group = here[blk]
        lo, hi = _span(group, table)
        for hg in range(H // HG):
            q = _stack(q_out, rows, hg * HG, HG)
            width = HG * GROUP
            pos = group * GROUP + lax.rem(
                lax.broadcasted_iota(jnp.int32, (1, width), 1), GROUP
            )
            start = _starts(pos, table)

            def score(t, top):
                at = pl.ds(pl.multiple_of(t * TILE, TILE), TILE)
                s = _nt(sorted_kv[at, :HD], q)
                key = t * TILE + lax.broadcasted_iota(jnp.int32, (TILE, width), 0)
                s = jnp.where((key >= start) & (key <= pos), s, -1e30)
                scores[at, :] = s
                return jnp.maximum(top, jnp.max(s, axis=0, keepdims=True))

            top = lax.fori_loop(lo, hi, score, jnp.full((1, width), -1e30, F32))

            def weigh(t, carry):
                total, summed = carry
                at = pl.ds(pl.multiple_of(t * TILE, TILE), TILE)
                p = jnp.exp(scores[at, :] - top)
                total = total + jnp.sum(p, axis=0, keepdims=True)
                return total, summed + _tn(sorted_kv[at, HD:], p.astype(BF))

            total, summed = lax.fori_loop(
                lo, hi, weigh, (jnp.zeros((1, width), F32), jnp.zeros((HD, width), F32))
            )
            lse_out[blk, hg : hg + 1, :] = top + jnp.log(total)
            att = jnp.transpose(summed / total)
            for h in range(HG):
                head = hg * HG + h
                piece = att[h * GROUP : (h + 1) * GROUP, :]
                att_out[rows, head * HD : (head + 1) * HD] = piece
                lanes = slice((head % per_chunk) * HD, (head % per_chunk + 1) * HD)
                chunk_out[head // per_chunk, rows, lanes] = piece.astype(BF)


def attend(net, table, order, here, me, low, cos, sin, kv, pieces):
    tokens, low_rank = low.shape
    slot_rows = kv.shape[0]
    ways = 2 * net.S
    return _call(
        functools.partial(attend_kernel, net, len(pieces)),
        "attend",
        (
            _shape(tokens, low_rank),
            _shape(tokens, H * HD),
            _shape(tokens, H * HD, dtype=F32),
            _shape(ways, tokens, H * HD // ways),
            _shape(2, H // HG, HG * GROUP, dtype=F32),
        ),
        [table, order, here, me, low, cos, sin, kv, *pieces],
        [
            pltpu.VMEM((low_rank, pieces[0].shape[1]), BF),
            pltpu.VMEM((slot_rows, 2 * HD), BF),
            pltpu.VMEM((slot_rows, HG * GROUP), F32),
        ],
    )


def _owner(net, me, place, other):
    slot = jnp.bitwise_xor(me[0], place) if net.S == 4 else place
    return slot * 2 + (1 - me[1] if other else me[1])


def out_kernel(net, me, heads, out_rows, *parts):
    tokens, size = heads.shape[1:]
    weight = out_rows[pl.ds(pl.multiple_of(me[1] * size, size), size), :]
    for side in (1, 0):
        for first in range(0, net.S, 2):
            rows = jnp.concatenate(
                [heads[_owner(net, me, first + k, side == 1)] for k in range(2)], axis=0
            )
            got = jnp.dot(rows, weight, preferred_element_type=F32).astype(BF)
            for k in range(2):
                parts[side * net.S + first + k][...] = got[k * tokens : (k + 1) * tokens, :]


def out_forward(net, me, heads, out_rows):
    tokens = heads.shape[1]
    return _call(
        functools.partial(out_kernel, net),
        "out_forward",
        [_shape(tokens, out_rows.shape[1])] * (2 * net.S),
        [me, heads, out_rows],
    )


def _blocks(net, n):
    piece = n // (net.S * net.Z)
    return piece, [s * net.Z + z for z in range(net.Z) for s in range(net.S)]


def middle_kernel(net, x, gains, left, left_last, right, right_last, mid_out, h2_out):
    half = left.shape[0]
    for rows, one, two in ((slice(0, half), left, left_last), (slice(half, 2 * half), right, right_last)):
        mid = x[rows, :].astype(F32) + (one[...].astype(F32) + two[...].astype(F32))
        mid_out[rows, :] = mid
        h2 = (mid * _mean_scale(mid) * gains[1:2, :]).astype(BF)
        piece, places = _blocks(net, mid.shape[1])
        for k, place in enumerate(places):
            h2_out[rows, k * piece : (k + 1) * piece] = h2[:, place * piece : (place + 1) * piece]


def middle_forward(net, x, gains, parts):
    return _call(
        functools.partial(middle_kernel, net),
        "middle_forward",
        (_shape(*x.shape, dtype=F32), _shape(*x.shape)),
        [x, gains, *parts],
    )


def middle_back_kernel(net, mid_ref, gains, cot, left, left_last, right, right_last, grad_out, low_out, gain_out):
    half = left.shape[0]
    total = jnp.zeros((1, mid_ref.shape[1]), F32)
    gain = gains[1:2, :]
    for rows, one, two in ((slice(0, half), left, left_last), (slice(half, 2 * half), right, right_last)):
        came = one[...].astype(F32) + two[...].astype(F32)
        piece, places = _blocks(net, came.shape[1])
        back = [None] * len(places)
        for k, place in enumerate(places):
            back[place] = came[:, k * piece : (k + 1) * piece]
        upstream = jnp.concatenate(back, axis=1)
        mid = mid_ref[rows, :]
        scale = _mean_scale(mid)
        scaled = gain * upstream
        total = total + jnp.sum(upstream * mid * scale, axis=0, keepdims=True)
        inner = jnp.mean(scaled * mid, axis=1, keepdims=True)
        grad = cot[rows, :].astype(F32) + scale * scaled - mid * (scale * scale * scale * inner)
        grad_out[rows, :] = grad
        low_out[rows, :] = grad.astype(BF)
    gain_out[...] = jnp.broadcast_to(total, gain_out.shape)


def middle_back(net, mid, gains, cot, parts):
    return _call(
        functools.partial(middle_back_kernel, net),
        "middle_back",
        (_shape(*mid.shape, dtype=F32), _shape(*mid.shape), _shape(8, mid.shape[1], dtype=F32)),
        [mid, gains, cot, *parts],
    )


def _tiles(rows, size):
    tiles, held, left = [], [], size
    for k, n in enumerate(rows):
        first = 0
        while first < n:
            take = min(left, n - first)
            held.append((k, first, take))
            first, left = first + take, left - take
            if not left:
                tiles.append(held)
                held, left = [], size
    assert not held
    return tiles


def ffn_kernel(net, tiles, splits, me, *refs):
    count = len({k for tile in tiles for k, _, _ in tile})
    results = len({k for tile in splits for k, _, _ in tile})
    h, d = refs[:count], refs[count : 2 * count]
    gu_w, down_rows = refs[2 * count : 2 * count + 2]
    outs = refs[2 * count + 2 : 2 * count + 2 + results]
    h_out, d_out, hid_out, dgu_out = refs[2 * count + 2 + results : 2 * count + 6 + results]
    hv, dv, gv, wv, xv, hidv, dguv, sem_in, sem_out = refs[2 * count + 6 + results :]
    wide = hid_out.shape[1]
    size = hv.shape[1]

    def fetch(t, sources, target, sem):
        copies, at = [], 0
        for n, (k, first, rows) in enumerate(tiles[t]):
            copies.append(
                pltpu.make_async_copy(
                    sources[k].at[pl.ds(first, rows)], target.at[t, pl.ds(at, rows)], sem.at[n]
                )
            )
            at += rows
        return copies

    gu_copy = pltpu.make_async_copy(gu_w, gv, sem_in.at[0, 0, 0])
    down_copy = pltpu.make_async_copy(
        down_rows.at[pl.ds(pl.multiple_of(me[1] * wide, 16), wide)], wv, sem_in.at[0, 0, 1]
    )
    h_copies = [fetch(t, h, hv, sem_in.at[1, t]) for t in range(len(tiles))]
    d_copies = [fetch(t, d, dv, sem_in.at[2, t]) for t in range(len(tiles))]
    for c in d_copies[0] + [down_copy] + h_copies[0] + [gu_copy]:
        c.start()
    for t in range(1, len(tiles)):
        for c in d_copies[t] + h_copies[t]:
            c.start()
    sent = []

    def send(source, target, sem):
        copy = pltpu.make_async_copy(source, target, sem)
        copy.start()
        sent.append(copy)

    for t in range(len(tiles)):
        rows = pl.ds(t * size, size)
        for c in d_copies[t] + ([down_copy] if t == 0 else []):
            c.wait()
        send(dv.at[t], d_out.at[rows], sem_out.at[t, 0])
        grad = _nt(dv[t], wv[...])
        for c in h_copies[t] + ([gu_copy] if t == 0 else []):
            c.wait()
        send(hv.at[t], h_out.at[rows], sem_out.at[t, 1])
        both = jnp.dot(hv[t], gv[...], preferred_element_type=F32)
        gate = both[:, :wide]
        up = both[:, wide:]
        sigma = jax.nn.sigmoid(gate)
        silu = gate * sigma
        hidv[t] = (silu * up).astype(BF)
        send(hidv.at[t], hid_out.at[rows], sem_out.at[t, 2])
        dguv[t] = jnp.concatenate(
            [grad * up * sigma * (1.0 + gate * (1.0 - sigma)), grad * silu], axis=1
        ).astype(BF)
        send(dguv.at[t], dgu_out.at[rows], sem_out.at[t, 3])
        xv[t] = _nt(dguv[t], gv[...]).astype(BF)
        at = 0
        for n, (k, first, take) in enumerate(splits[t]):
            send(xv.at[t, pl.ds(at, take)], outs[k].at[pl.ds(first, take)], sem_out.at[t, 4 + n])
            at += take
    for copy in sent:
        copy.wait()


def ffn(net, me, h, d, gu_w, down_rows, tokens):
    width = gu_w.shape[0]
    wide = gu_w.shape[1] // 2
    size = 2 * tokens
    tiles = _tiles([a.shape[0] for a in h], size)
    out_rows = [tokens] * (2 * net.S)
    splits = _tiles(out_rows, size)
    steps = len(tiles)
    every = steps * size
    return _call(
        functools.partial(ffn_kernel, net, tiles, splits),
        "ffn",
        [_shape(n, width) for n in out_rows]
        + [_shape(every, n) for n in (width, width, wide, 2 * wide)],
        [me, *h, *d, gu_w, down_rows],
        [
            pltpu.VMEM((steps, size, width), BF),
            pltpu.VMEM((steps, size, width), BF),
            pltpu.VMEM((width, 2 * wide), BF),
            pltpu.VMEM((wide, width), BF),
            pltpu.VMEM((steps, size, width), BF),
            pltpu.VMEM((steps, size, wide), BF),
            pltpu.VMEM((steps, size, 2 * wide), BF),
            pltpu.SemaphoreType.DMA((3, steps, 5)),
            pltpu.SemaphoreType.DMA((steps, 8)),
        ],
        memory=pl.ANY,
    )


def out_back_kernel(net, count, me, out_rows, *refs):
    rows_in, (heads_out,) = refs[:count], refs[count:]
    ways, tokens, size = heads_out.shape
    weight = out_rows[pl.ds(pl.multiple_of(me[1] * size, size), size), :]
    group = count // 2
    for side in range(2):
        rows = jnp.concatenate([ref[...] for ref in rows_in[side * group : (side + 1) * group]], axis=0)
        got = _nt(rows, weight).astype(BF)
        for place in range(net.S):
            heads_out[_owner(net, me, place, side == 0)] = got[place * tokens : (place + 1) * tokens, :]


def out_back(net, me, out_rows, rows, tokens):
    ways = 2 * net.S
    return _call(
        functools.partial(out_back_kernel, net, len(rows)),
        "out_back",
        _shape(ways, tokens, out_rows.shape[0] // 2),
        [me, out_rows, *rows],
    )


def out_grad_kernel(net, count, me, heads, *refs):
    rows_in, (grad_out,) = refs[:count], refs[count:]
    group = count // 2
    total = None
    for side in range(2):
        left = jnp.concatenate(
            [heads[_owner(net, me, place, side == 0)] for place in range(net.S)], axis=0
        )
        right = jnp.concatenate([ref[...] for ref in rows_in[side * group : (side + 1) * group]], axis=0)
        part = _tn(left, right)
        total = part if total is None else total + part
    grad_out[...] = total.astype(BF)


def out_weight_grad(net, me, heads, rows):
    return _call(
        functools.partial(out_grad_kernel, net, len(rows)),
        "out_weight_grad",
        _shape(heads.shape[2], rows[0].shape[1]),
        [me, heads, *rows],
    )


def back_kernel(table, order, here, q_in, grad, att, lse, cos, sin, kv, dq_out, dkv_out, sorted_kv, dk, dv):
    _sort_keys(order, kv, sorted_kv)
    dk[...] = jnp.zeros_like(dk)
    dv[...] = jnp.zeros_like(dv)
    scale = 1.0 / math.sqrt(HD)
    half = HD // 2
    per_chunk = grad.shape[2] // HD
    for blk in range(2):
        rows = slice(blk * GROUP, (blk + 1) * GROUP)
        group = here[blk]
        lo, hi = _span(group, table)
        cosine, sine = cos[rows, :], sin[rows, :]
        for hg in range(H // HG):
            width = HG * GROUP
            q = _stack(q_in, rows, hg * HG, HG)
            da = jnp.concatenate(
                [
                    grad[
                        head // per_chunk,
                        rows,
                        (head % per_chunk) * HD : (head % per_chunk + 1) * HD,
                    ]
                    for head in range(hg * HG, (hg + 1) * HG)
                ],
                axis=0,
            )
            kept = _stack(att, rows, hg * HG, HG)
            delta = jnp.sum(da.astype(F32) * kept, axis=1, keepdims=True)
            delta = jnp.transpose(jnp.broadcast_to(delta, (width, 128)))[:1, :]
            shift = lse[blk, hg : hg + 1, :]
            pos = group * GROUP + lax.rem(
                lax.broadcasted_iota(jnp.int32, (1, width), 1), GROUP
            )
            start = _starts(pos, table)

            def step(t, dq):
                at = pl.ds(pl.multiple_of(t * TILE, TILE), TILE)
                k = sorted_kv[at, :HD]
                s = _nt(k, q)
                key = t * TILE + lax.broadcasted_iota(jnp.int32, (TILE, width), 0)
                p = jnp.where((key >= start) & (key <= pos), jnp.exp(s - shift), 0.0)
                dp = _nt(sorted_kv[at, HD:], da)
                ds = (p * (dp - delta)).astype(BF)
                dv[at, :] += jnp.dot(p.astype(BF), da, preferred_element_type=F32)
                dk[at, :] += jnp.dot(ds, q, preferred_element_type=F32)
                return dq + _tn(k, ds)

            dq = jnp.transpose(lax.fori_loop(lo, hi, step, jnp.zeros((HD, width), F32)))
            dq = dq * scale
            for h in range(HG):
                head = hg * HG + h
                a = dq[h * GROUP : (h + 1) * GROUP, :half]
                b = dq[h * GROUP : (h + 1) * GROUP, half:]
                dq_out[rows, head * HD : head * HD + half] = (a * cosine + b * sine).astype(BF)
                dq_out[rows, head * HD + half : (head + 1) * HD] = (
                    b * cosine - a * sine
                ).astype(BF)
    for b in range(kv.shape[0] // GROUP):
        at = pl.ds(pl.multiple_of(order[b] * GROUP, GROUP), GROUP)
        dkv_out[b * GROUP : (b + 1) * GROUP, :HD] = dk[at, :].astype(BF)
        dkv_out[b * GROUP : (b + 1) * GROUP, HD:] = dv[at, :].astype(BF)


def attend_back(table, order, here, q, grad, att, lse, cos, sin, kv):
    slot_rows = kv.shape[0]
    return _call(
        back_kernel,
        "attend_back",
        (_shape(*q.shape), _shape(slot_rows, 2 * HD)),
        [table, order, here, q, grad, att, lse, cos, sin, kv],
        [
            pltpu.VMEM((slot_rows, 2 * HD), BF),
            pltpu.VMEM((slot_rows, HD), F32),
            pltpu.VMEM((slot_rows, HD), F32),
        ],
    )


def up_back_kernel(net, count, results, me, dq, cqn, low_ref, *refs):
    pieces, outs = refs[:count], refs[count : count + results]
    low_grad_out, up_q, grad = refs[count + results :]
    _join(net, me, pieces, up_q)
    wide = dq.shape[1]
    gain = jnp.transpose(up_q[:, wide:].astype(F32))[:1, :]
    upstream = _nt(dq[...], up_q[:, :wide])
    low = low_ref[...]
    scale = _mean_scale(low)
    gain_grad = jnp.sum(upstream * low * scale, axis=0, keepdims=True)
    scaled = gain * upstream
    inner = jnp.mean(scaled * low, axis=1, keepdims=True)
    low_grad_out[...] = (scale * scaled - low * (scale * scale * scale * inner)).astype(BF)
    step = 1024
    for first in range(0, wide, step):
        grad[:, first : first + step] = _tn(cqn[...], dq[:, first : first + step]).astype(BF)
    grad[:, wide:] = jnp.transpose(
        jnp.broadcast_to(gain_grad, (128, gain_grad.shape[1]))
    ).astype(BF)
    _part(net, me, grad, outs)


def up_back(net, me, dq, cqn, low, pieces):
    tokens, low_rank = low.shape
    wide = pieces[0].shape[1]
    outs = _out_pieces(net, low_rank, wide)
    *parts, grad = _call(
        functools.partial(up_back_kernel, net, len(pieces), len(outs)),
        "up_back",
        outs + [_shape(tokens, low_rank)],
        [me, dq, cqn, low, *pieces],
        [pltpu.VMEM((low_rank, wide), BF), pltpu.VMEM((low_rank, wide), BF)],
    )
    return parts, grad


def _out_pieces(net, rows, wide):
    if not net.whole_pieces(rows):
        return [_shape(rows // (2 * net.S), wide)] * (2 * net.S)
    return [_shape(rows, wide)]


def project_back_kernel(net, count, results, me, x_ref, low_grad, both, cos, sin, mid_grad, gains, mid_gain, *refs):
    pieces, outs = refs[:count], refs[count : count + results]
    in_out, whole, grad = refs[count + results :]
    _join(net, me, pieces, whole)
    width = whole.shape[0]
    low_rank = low_grad.shape[1]
    last = low_rank + 2 * HD
    half = HD // 2
    a, b = both[:, :half].astype(F32), both[:, half:HD].astype(F32)
    upstream_parts = jnp.concatenate(
        [
            low_grad[...],
            (a * cos[...] + b * sin[...]).astype(BF),
            (b * cos[...] - a * sin[...]).astype(BF),
            both[:, HD:].astype(BF),
        ],
        axis=1,
    )
    x = x_ref[...].astype(F32)
    scale = _mean_scale(x)
    gain = gains[:1, :]
    normed = (x * scale * gain).astype(BF)
    for first in range(0, last, 512):
        grad[:, first : first + 512] = _tn(normed, upstream_parts[:, first : first + 512]).astype(BF)
    upstream = _nt(upstream_parts, whole[:, :last])
    gain_grad = jnp.sum(upstream * x * scale, axis=0, keepdims=True)
    scaled = gain * upstream
    inner = jnp.mean(scaled * x, axis=1, keepdims=True)
    in_out[...] = (mid_grad[...] + scale * scaled - x * (scale * scale * scale * inner)).astype(BF)
    tall = lax.broadcasted_iota(jnp.int32, (128, width), 0)
    both_gains = jnp.where(
        tall == 0, jnp.broadcast_to(gain_grad, (128, width)),
        jnp.broadcast_to(mid_gain[:1, :], (128, width)),
    )
    grad[:, last:] = jnp.transpose(both_gains).astype(BF)
    _part(net, me, grad, outs)


def project_back(net, me, x, low_grad, both, cos, sin, mid_grad, gains, mid_gain, pieces):
    tokens, width = x.shape
    wide = pieces[0].shape[1]
    outs = _out_pieces(net, width, wide)
    *parts, in_grad = _call(
        functools.partial(project_back_kernel, net, len(pieces), len(outs)),
        "project_back",
        outs + [_shape(tokens, width)],
        [me, x, low_grad, both, cos, sin, mid_grad, gains, mid_gain, *pieces],
        [pltpu.VMEM((width, wide), BF), pltpu.VMEM((width, wide), BF)],
    )
    return parts, in_grad


def share_kernel(net, me, hidden, down_rows, *parts):
    tokens = parts[0].shape[0]
    wide = hidden.shape[1]
    weight = down_rows[pl.ds(pl.multiple_of(me[1] * wide, 16), wide), :]
    for first in range(0, len(parts), 2):
        rows = hidden[first * tokens : (first + 2) * tokens, :]
        got = jnp.dot(rows, weight, preferred_element_type=F32).astype(BF)
        for k in range(2):
            parts[first + k][...] = got[k * tokens : (k + 1) * tokens, :]


def down_share(net, me, hidden, down_rows, tokens):
    return _call(
        functools.partial(share_kernel, net),
        "down_share",
        [_shape(tokens, down_rows.shape[1])] * (2 * net.S),
        [me, hidden, down_rows],
    )


def body(
    net,
    hidden_in, seq_lens, group_order, attn_gain, wq_down, q_gain, wq_up, w_key, w_value, w_out,
    ffn_gain, w_gate, w_up, w_down, out_grad,
):
    lengths = seq_lens[0]
    order = group_order[0]
    tokens = hidden_in.shape[0]
    low_rank = wq_up.shape[0] * net.S * net.Z * 2
    last = low_rank + 2 * HD
    me = net.me()
    place = lax.axis_index("z") * 2 + lax.axis_index("c")
    rows_here = place * tokens + jnp.arange(tokens, dtype=jnp.int32)
    seq_pos, valid = place_info(rows_here, order, lengths, tokens)
    cosine, sine = rope_tables(seq_pos, HD)
    table = jnp.concatenate([jnp.cumsum(lengths), lengths]).astype(jnp.int32)
    here = lax.dynamic_slice_in_dim(order, 2 * place, 2, 0)
    kept = {}

    gains = column(attn_gain) + jnp.roll(column(ffn_gain), 1, axis=1)
    first_z = net.z_gather(jnp.concatenate([wq_down, w_key, w_value, gains], axis=1))
    up_z = net.z_gather(jnp.concatenate([wq_up, column(q_gain)], axis=1))
    out_rows = net.rows_gather(w_out)
    down_rows = net.rows_gather(w_down)

    def first_one(*moved):
        *moved, kept["up_z"] = tie(*moved, up_z)
        return moved

    first_pieces = net.weight_pieces(net.spread(first_z, (first_one,)))

    w_gate, w_up, *_ = tie(w_gate, w_up, *first_pieces)
    gu_mine = net.cols_exchange(w_gate, w_up)

    def up_one(*moved):
        kept["gu_mine"], *moved = tie(gu_mine, *moved)
        return moved

    up_pieces = net.weight_pieces(net.spread(kept["up_z"], (up_one,)))

    query_low, kv, gains = project(net, me, hidden_in, cosine, sine, first_pieces, low_rank)
    kv, out_rows = tie(kv, out_rows)
    both = net.rows_gather(kv)
    gu_chunk = net.z_gather(kept["gu_mine"])
    cot = (out_grad.astype(F32) * valid[:, None].astype(F32)).astype(BF)
    cot, *_ = tie(cot, *up_pieces)

    def cot_one(*moved):
        kept["attend"] = attend(
            net, table, order, here, me, query_low, cosine, sine, both, up_pieces
        )
        *kept["attend"], a, b = tie(*kept["attend"], *moved, *moved[: 2 - len(moved)])
        return [a, b][: len(moved)]

    def cot_two(*moved):
        heads = net.exchange(kept["attend"][3])
        parts = out_forward(net, me, heads, out_rows)
        kept["heads"] = heads
        done = tie(*moved, *parts)
        kept["out_parts"] = done[len(moved) :]
        return done[: len(moved)]

    cot_same = net.spread(cot, (cot_one, cot_two))
    cot_other = net.swap_all(cot_same)
    query_normed, query_rows, attended, _, log_total = kept["attend"]
    heads = kept["heads"]
    out_parts = kept["out_parts"]
    middle, normed_two = middle_forward(
        net, hidden_in, gains, net.collect(out_parts[: net.S], out_parts[net.S :])
    )

    two_same = net.spread(normed_two)
    two_all = [*net.swap_all(two_same), *two_same]
    cot_all = [*cot_other, *cot_same]
    *back_parts, two_rows, cot_rows, hidden, gu_grad = ffn(
        net, me, two_all, cot_all, gu_chunk, down_rows, tokens
    )

    def back_one(*came):
        *_, kept["hidden"], kept["gu_grad"] = tie(*came, hidden, gu_grad)
        kept["grad_down"] = net.rows_return(contract_first(kept["hidden"], cot_rows).astype(BF))
        return came

    def back_two(*moved):
        *moved, kept["grad_down"] = tie(*moved, kept["grad_down"])
        gu_grad, *_ = tie(kept["gu_grad"], *moved)
        kept["grad_gu"] = contract_first(two_rows, gu_grad).astype(BF)
        return moved

    def back_three(*moved):
        *moved, kept["grad_gu"] = tie(*moved, kept["grad_gu"])
        return moved

    middle_grad, middle_low, middle_gain = middle_back(
        net,
        middle,
        gains,
        cot,
        net.collect(
            back_parts[net.S :], back_parts[: net.S], (back_one, back_two, back_three)
        ),
    )
    grad_down = net.z_scatter(kept["grad_down"])
    grad_gu = net.z_scatter(kept["grad_gu"])

    def middle_one(*moved):
        hidden, *_ = tie(kept["hidden"], middle_low)
        shares = down_share(net, me, hidden, down_rows, tokens)
        done = tie(*moved, *shares)
        kept["shares"] = done[len(moved) :]
        return done[: len(moved)]

    def middle_two(*moved):
        *moved, kept["grad_down"] = tie(*moved, grad_down)
        return moved

    middle_same = net.spread(middle_low, (middle_one, middle_two))
    grad_down = kept["grad_down"].astype(F32)
    middle_all = [*net.swap_all(middle_same), *middle_same]
    heads_grad = net.exchange(out_back(net, me, out_rows, middle_all, tokens))
    grad_out = net.rows_return(out_weight_grad(net, me, heads, middle_all))
    heads_grad, grad_out, *shares = tie(heads_grad, grad_out, *kept["shares"])
    grad_out = net.z_scatter(grad_out)

    def result_two(*moved):
        backs = attend_back(
            table, order, here, query_rows, heads_grad, attended, log_total, cosine, sine, both
        )
        *moved, kept["query_pre"], kept["both_grads"], kept["grad_gu"] = tie(
            *moved, *backs, grad_gu
        )
        return moved

    upper, upper_last, lower, lower_last = net.collect(
        shares[net.S :], shares[: net.S], (None, result_two)
    )
    layer_out = (
        middle
        + jnp.concatenate(
            [upper + upper_last.astype(F32), lower + lower_last.astype(F32)], axis=0
        )
    ).astype(BF)
    both_sum = lax.psum_scatter(kept["both_grads"], ("z", "c"), scatter_dimension=0, tiled=True)
    up_parts, low_grad = up_back(net, me, kept["query_pre"], query_normed, query_low, up_pieces)

    def whole(parts):
        upper, upper_last, lower, lower_last = parts
        return net.z_scatter(
            jnp.concatenate(
                [upper + upper_last.astype(F32), lower + lower_last.astype(F32)], axis=0
            )
        ).astype(F32)

    up_out = whole(net.collect(*net.weight_sides(up_parts)))
    first_parts, in_grad = project_back(
        net, me, hidden_in, low_grad, both_sum, cosine, sine, middle_grad, gains, middle_gain,
        first_pieces,
    )

    def first_two(*moved):
        *moved, kept["grad_out"] = tie(*moved, grad_out)
        return moved

    first_out = whole(net.collect(*net.weight_sides(first_parts), (None, first_two)))
    grad_out = kept["grad_out"].astype(F32)
    grad_gate, grad_upward = net.cols_return(kept["grad_gu"])
    return (
        layer_out,
        in_grad,
        first_out[:, last],
        first_out[:, :low_rank],
        up_out[:, H * HD],
        up_out[:, : H * HD],
        first_out[:, low_rank : low_rank + HD],
        first_out[:, low_rank + HD : last],
        grad_out,
        first_out[:, last + 1],
        grad_gate,
        grad_upward,
        grad_down,
    )


def solution(mesh):
    slots, seq = mesh.devices.shape
    fine = Mesh(mesh.devices.reshape(slots, seq // 2, 2), ("slot", "z", "c"))
    every = ("slot", "z", "c")
    matrix = P(every, None)
    vector = P(every)
    net = Net(slots, seq // 2)
    return jax.shard_map(
        functools.partial(body, net),
        mesh=fine,
        in_specs=(
            matrix, P("slot", None), P("slot", None), vector, matrix, vector, matrix, matrix,
            matrix, matrix, vector, matrix, matrix, matrix, matrix,
        ),
        out_specs=(
            matrix, matrix, vector, matrix, vector, matrix, matrix, matrix, matrix, vector,
            matrix, matrix, matrix,
        ),
        check_vma=False,
    )
```

```python
import functools
import math

import jax
import jax.numpy as jnp
from jax import lax
from jax.experimental import pallas as pl
from jax.experimental.pallas import tpu as pltpu
from jax.sharding import Mesh
from jax.sharding import PartitionSpec as P

H = 16
HD = 256
GROUP = 96
TILE = 256
HG = 8
VMEM_BYTES = 60 << 20

EPS = 1e-05
ROPE_BASE = 10000.0
BF = jnp.bfloat16
F32 = jnp.float32


class Net:
    def __init__(self, slots, depth):
        self.S = slots
        self.Z = depth

    def me(self):
        return jnp.stack([lax.axis_index("slot"), lax.axis_index("c")]).astype(jnp.int32)

    def whole_pieces(self, rows):
        return self.S != 4

    def segments(self, n):
        if self.S != 4:
            return [(0, 0, n)]
        half = n // 2
        return [(0, 0, n), (1, 0, n), (2, 0, n), (3, 0, half), (3, half, n - half)]

    def swap_c(self, a):
        return lax.ppermute(a, "c", [(0, 1), (1, 0)])

    def swap_x(self, a):
        return lax.ppermute(a, "slot", [(0, 1), (1, 0), (2, 3), (3, 2)])

    def swap_y(self, a):
        return lax.ppermute(a, "slot", [(0, 2), (2, 0), (1, 3), (3, 1)])

    def spread(self, a, during=()):
        first, second = [*during, None, None][:2]
        if self.S != 4:
            a = lax.all_gather(a, "slot", axis=0, tiled=True)
            for step in (first, second):
                if step is not None:
                    (a,) = step(a)
            return [a]
        half = a.shape[0] // 2
        ax = self.swap_x(a)
        ay = self.swap_y(a)
        if first is not None:
            ax, ay = first(ax, ay)
        d0 = self.swap_y(ax[:half])
        d1 = self.swap_x(ay[half:])
        if second is not None:
            d0, d1 = second(d0, d1)
        return [a, ax, ay, d0, d1]

    def swap_all(self, pieces):
        return [self.swap_c(a) for a in pieces]

    def weight_pieces(self, same):
        other = self.swap_all(same)
        if self.S == 4:
            return [*same, *other]
        n = same[0].shape[1]
        r = same[0].shape[0] // (self.S * self.Z)
        first = lax.axis_index("c") == 0
        same = same[0].reshape(self.S, self.Z, 1, r, n)
        other = other[0].reshape(self.S, self.Z, 1, r, n)
        pair = [jnp.where(first, same, other), jnp.where(first, other, same)]
        return [jnp.concatenate(pair, axis=2).reshape(-1, n)]

    def weight_sides(self, parts):
        if self.S == 4:
            return parts[:4], parts[4:]
        n = parts[0].shape[1]
        whole = parts[0].reshape(self.S, self.Z, 2, -1, n)
        r = whole.shape[3]
        core = lax.axis_index("c")
        return tuple(
            [
                lax.dynamic_slice_in_dim(whole[slot], k, 1, 1).reshape(self.Z * r, n)
                for slot in range(self.S)
            ]
            for k in (core, 1 - core)
        )

    def collect(self, same, other, during=()):
        first, second, third = [*during, None, None, None][:3]
        came = self.swap_all(other)
        if first is not None:
            came = first(*came)
        held = [a.astype(F32) + b.astype(F32) for a, b in zip(same, came)]
        half = same[0].shape[0] // 2
        if self.S != 4:
            total = jnp.concatenate(held, axis=0).astype(BF)
            for step in (second, third):
                if step is not None:
                    (total,) = step(total)
            total = lax.psum_scatter(total, "slot", scatter_dimension=0, tiled=True)
            upper, lower = total[:half].astype(F32), total[half:].astype(F32)
            return [upper, jnp.zeros_like(total[:half]), lower, jnp.zeros_like(total[half:])]
        via_x = self.swap_x(jnp.concatenate([held[1][:half], held[3][:half]], axis=0).astype(BF))
        via_y = self.swap_y(jnp.concatenate([held[2][half:], held[3][half:]], axis=0).astype(BF))
        if second is not None:
            via_x, via_y = second(via_x, via_y)
        via_x, via_y = via_x.astype(F32), via_y.astype(F32)
        upper = held[0][:half] + via_x[:half]
        lower = held[0][half:] + via_y[: via_y.shape[0] // 2]
        upper_last = self.swap_y((held[2][:half] + via_x[half:]).astype(BF))
        lower_last = self.swap_x((held[1][half:] + via_y[via_y.shape[0] // 2 :]).astype(BF))
        if third is not None:
            upper_last, lower_last = third(upper_last, lower_last)
        return [upper, upper_last, lower, lower_last]

    def z_gather(self, w):
        return lax.all_gather(w, "z", axis=0, tiled=True)

    def z_scatter(self, g):
        return lax.psum_scatter(g.astype(BF), "z", scatter_dimension=0, tiled=True)

    def rows_gather(self, w):
        return lax.all_gather(w, ("z", "c"), axis=0, tiled=True)

    def rows_parted(self, g):
        n = g.shape[1]
        core = lax.axis_index("c")
        parts = g.reshape(self.Z // 2, 2, -1, n)
        return [
            lax.dynamic_slice_in_dim(parts, k, 1, 1).reshape(-1, n) for k in (core, 1 - core)
        ]

    def rows_return(self, mine, sent):
        came = self.swap_c(sent)
        first = lax.axis_index("c") == 0
        return jnp.concatenate(
            [jnp.where(first, mine, came), jnp.where(first, came, mine)], axis=0
        )

    def cols_exchange(self, gate, up):
        r, n = gate.shape
        ways = 2 * self.S
        parts = jnp.concatenate(
            [gate.reshape(r, ways, n // ways), up.reshape(r, ways, n // ways)], axis=2
        ).transpose(1, 0, 2)
        return self.exchange(parts).reshape(ways * r, 2 * n // ways)

    def cols_return(self, mine):
        ways = 2 * self.S
        m = mine.shape[1] // 2
        parts = self.exchange(mine.reshape(ways, -1, 2 * m)).transpose(1, 0, 2)
        r = parts.shape[0]
        return (
            parts[:, :, :m].reshape(r, ways * m).astype(F32),
            parts[:, :, m:].reshape(r, ways * m).astype(F32),
        )

    def exchange(self, a):
        return lax.all_to_all(a, ("slot", "c"), 0, 0, tiled=True)

    def exchange_pieces(self, pieces):
        if self.S == 4:
            ways = 2 * self.S
            moved = [pieces[0]]
            for number in range(1, ways):
                step = 2 * (number % self.S) + number // self.S
                moved.append(
                    lax.ppermute(pieces[number], ("slot", "c"), [(i, i ^ step) for i in range(ways)])
                )
            return moved
        first = lax.axis_index("c") == 0
        same, other = jnp.stack(pieces[: self.S]), jnp.stack(pieces[self.S :])
        pair = jnp.stack([jnp.where(first, same, other), jnp.where(first, other, same)], axis=1)
        pair = self.exchange(pair.reshape(2 * self.S, *pieces[0].shape))
        low, high = pair[0::2], pair[1::2]
        return [*jnp.where(first, low, high), *jnp.where(first, high, low)]


def tie(*arrays):
    return lax.optimization_barrier(arrays)


def column(a):
    return jnp.pad(a.reshape(-1, 1), ((0, 0), (0, 127)))


def place_info(row_index, order, lengths, tokens):
    device = row_index // tokens
    local = row_index % tokens
    pick = 2 * device + local // GROUP
    table = jnp.arange(order.shape[0], dtype=jnp.int32)
    group_id = jnp.sum(jnp.where(pick[:, None] == table[None, :], order[None, :], 0), axis=1)
    slot_pos = group_id * GROUP + local % GROUP
    ends = jnp.cumsum(lengths)
    passed = slot_pos[:, None] >= ends[None, :]
    segment = jnp.sum(passed.astype(jnp.int32), axis=1)
    start = jnp.sum(jnp.where(passed, lengths[None, :], 0), axis=1)
    return (slot_pos - start, segment < lengths.shape[0])


def rope_tables(position, width):
    half = width // 2
    freq = ROPE_BASE ** (-2.0 * jnp.arange(half, dtype=F32) / width)
    angle = position.astype(F32)[:, None] * freq[None, :]
    return (jnp.cos(angle), jnp.sin(angle))


def _call(kernel, name, out_shape, args, scratch=(), memory=None):
    specs = [
        pl.BlockSpec(
            memory_space=pltpu.SMEM
            if a.dtype == jnp.int32 and a.ndim == 1
            else (memory or pltpu.VMEM)
        )
        for a in args
    ]
    many = isinstance(out_shape, (tuple, list))
    out_specs = [pl.BlockSpec(memory_space=memory or pltpu.VMEM)] * (len(out_shape) if many else 1)
    return pl.pallas_call(
        kernel,
        out_shape=out_shape,
        in_specs=specs,
        out_specs=out_specs if many else out_specs[0],
        scratch_shapes=list(scratch),
        compiler_params=pltpu.CompilerParams(vmem_limit_bytes=VMEM_BYTES),
        cost_estimate=pl.CostEstimate(flops=1, bytes_accessed=1, transcendentals=0),
        name=name,
    )(*args)


def _shape(*dims, dtype=BF):
    return jax.ShapeDtypeStruct(dims, dtype)


def _nt(a, b):
    return lax.dot_general(a, b, (((1,), (1,)), ((), ())), preferred_element_type=F32)


def _tn(a, b):
    return lax.dot_general(a, b, (((0,), (0,)), ((), ())), preferred_element_type=F32)


def _row_place(net, me, place, z, other, r):
    slot = jnp.bitwise_xor(me[0], place) if net.S == 4 else place
    core = 1 - me[1] if other else me[1]
    return pl.multiple_of(((slot * net.Z + z) * 2 + core) * r, r)


def _join(net, me, pieces, whole):
    if len(pieces) == 1:
        whole[...] = pieces[0][...]
        return
    r = whole.shape[0] // (net.S * net.Z * 2)
    for side in range(2):
        for (place, first, count), ref in zip(net.segments(net.Z * r), pieces[side * 5 : side * 5 + 5]):
            for k in range(count // r):
                at = _row_place(net, me, place, first // r + k, side == 1, r)
                whole[pl.ds(at, r), :] = ref[k * r : (k + 1) * r, :]


def _part(net, me, whole, pieces):
    if len(pieces) == 1:
        pieces[0][...] = whole[...]
        return
    r = whole.shape[0] // (net.S * net.Z * 2)
    for side in range(2):
        for place in range(net.S):
            for z in range(net.Z):
                at = _row_place(net, me, place, z, side == 1, r)
                pieces[side * net.S + place][z * r : (z + 1) * r, :] = whole[pl.ds(at, r), :]


def _mean_scale(values):
    return lax.rsqrt(jnp.mean(values * values, axis=1, keepdims=True) + EPS)


def project_kernel(net, count, me, x_ref, cos, sin, *refs):
    pieces, (low_out, kv_out, gain_out, whole) = refs[:count], refs[count:]
    _join(net, me, pieces, whole)
    width = whole.shape[0]
    low_rank = low_out.shape[1]
    last = low_rank + 2 * HD
    gains = jnp.transpose(whole[:, last:].astype(F32))
    gain_out[...] = gains[: gain_out.shape[0], :]
    x = x_ref[...].astype(F32)
    normed = (x * _mean_scale(x) * gains[:1, :]).astype(BF)
    low_out[...] = jnp.dot(normed, whole[:, :low_rank], preferred_element_type=F32)
    both = jnp.dot(normed, whole[:, low_rank:last], preferred_element_type=F32)
    half = HD // 2
    a, b = both[:, :half], both[:, half:HD]
    kv_out[:, :half] = (a * cos[...] - b * sin[...]).astype(BF)
    kv_out[:, half:HD] = (a * sin[...] + b * cos[...]).astype(BF)
    kv_out[:, HD:] = both[:, HD:].astype(BF)


def project(net, me, x, cos, sin, pieces, low_rank):
    tokens, width = x.shape
    wide = pieces[0].shape[1]
    return _call(
        functools.partial(project_kernel, net, len(pieces)),
        "project",
        (_shape(tokens, low_rank, dtype=F32), _shape(tokens, 2 * HD), _shape(8, width, dtype=F32)),
        [me, x, cos, sin, *pieces],
        [pltpu.VMEM((width, wide), BF)],
    )


def _starts(pos, table):
    start = jnp.zeros_like(pos)
    count = table.shape[0] // 2
    for k in range(count):
        start = start + jnp.where(pos >= table[k], table[count + k], 0)
    return start


def _start_of(pos, table):
    start = jnp.int32(0)
    count = table.shape[0] // 2
    for k in range(count):
        start = start + jnp.where(pos >= table[k], table[count + k], 0)
    return start


def _span(group, table):
    return _start_of(group * GROUP, table) // TILE, (group * GROUP + GROUP - 1) // TILE + 1


def _stack(ref, rows, first, heads):
    return jnp.concatenate(
        [ref[rows, (first + h) * HD : (first + h + 1) * HD] for h in range(heads)], axis=0
    )


def _sort_keys(order, kv, sorted_kv):
    for b in range(kv.shape[0] // GROUP):
        at = pl.ds(pl.multiple_of(order[b] * GROUP, GROUP), GROUP)
        sorted_kv[at, :] = kv[b * GROUP : (b + 1) * GROUP, :]


def _key_blocks(net, me, order):
    for side in range(2):
        core = me[1] if side == 0 else 1 - me[1]
        for k in range(2 * net.Z):
            group = order[2 * (2 * (k // 2) + core) + k % 2]
            at = pl.ds(pl.multiple_of(group * GROUP, GROUP), GROUP)
            yield side, slice(k * GROUP, (k + 1) * GROUP), at


def attend_kernel(net, count, table, order, here, me, low, gain, cos, sin, kv, *refs):
    pieces, parts = refs[:count], refs[count : count + 2 * net.S]
    cqn_out, q_out, att_out, lse_out, up_q, sorted_kv, scores, chunk_out = refs[
        count + 2 * net.S :
    ]
    _join(net, me, pieces, up_q)
    _sort_keys(order, kv, sorted_kv)
    cqn_out[...] = (low[...] * _mean_scale(low[...]) * gain[...]).astype(BF)
    scale = 1.0 / math.sqrt(HD)
    half = HD // 2
    per_chunk = chunk_out.shape[2] // HD
    for h in range(H):
        full = jnp.dot(
            cqn_out[...], up_q[:, h * HD : (h + 1) * HD], preferred_element_type=F32
        )
        a, b = full[:, :half], full[:, half:]
        q_out[:, h * HD : h * HD + half] = ((a * cos[...] - b * sin[...]) * scale).astype(BF)
        q_out[:, h * HD + half : (h + 1) * HD] = (
            (a * sin[...] + b * cos[...]) * scale
        ).astype(BF)
    for blk in range(2):
        rows = slice(blk * GROUP, (blk + 1) * GROUP)
        group = here[blk]
        lo, hi = _span(group, table)
        for hg in range(H // HG):
            q = _stack(q_out, rows, hg * HG, HG)
            width = HG * GROUP
            pos = group * GROUP + lax.rem(
                lax.broadcasted_iota(jnp.int32, (1, width), 1), GROUP
            )
            start = _starts(pos, table)

            def score(t, top):
                at = pl.ds(pl.multiple_of(t * TILE, TILE), TILE)
                s = _nt(sorted_kv[at, :HD], q)
                key = t * TILE + lax.broadcasted_iota(jnp.int32, (TILE, width), 0)
                s = jnp.where((key >= start) & (key <= pos), s, -1e30)
                scores[at, :] = s
                return jnp.maximum(top, jnp.max(s, axis=0, keepdims=True))

            top = lax.fori_loop(lo, hi, score, jnp.full((1, width), -1e30, F32))

            def weigh(t, carry):
                total, summed = carry
                at = pl.ds(pl.multiple_of(t * TILE, TILE), TILE)
                p = jnp.exp(scores[at, :] - top)
                total = total + jnp.sum(p, axis=0, keepdims=True)
                return total, summed + _tn(sorted_kv[at, HD:], p.astype(BF))

            total, summed = lax.fori_loop(
                lo, hi, weigh, (jnp.zeros((1, width), F32), jnp.zeros((HD, width), F32))
            )
            lse_out[blk, hg : hg + 1, :] = top + jnp.log(total)
            att = jnp.transpose(summed / total)
            for h in range(HG):
                head = hg * HG + h
                piece = att[h * GROUP : (h + 1) * GROUP, :]
                att_out[rows, head * HD : (head + 1) * HD] = piece
                lanes = slice((head % per_chunk) * HD, (head % per_chunk + 1) * HD)
                chunk_out[head // per_chunk, rows, lanes] = piece.astype(BF)
    for number, part in enumerate(parts):
        part[...] = chunk_out[_owner(net, me, number % net.S, number >= net.S)]


def attend(net, table, order, here, me, low, gain, cos, sin, kv, pieces):
    tokens, low_rank = low.shape
    slot_rows = kv.shape[0]
    ways = 2 * net.S
    return _call(
        functools.partial(attend_kernel, net, len(pieces)),
        "attend",
        [_shape(tokens, H * HD // ways)] * ways
        + [
            _shape(tokens, low_rank),
            _shape(tokens, H * HD),
            _shape(tokens, H * HD, dtype=F32),
            _shape(2, H // HG, HG * GROUP, dtype=F32),
        ],
        [table, order, here, me, low, gain, cos, sin, kv, *pieces],
        [
            pltpu.VMEM((low_rank, H * HD), BF),
            pltpu.VMEM((slot_rows, 2 * HD), BF),
            pltpu.VMEM((slot_rows, HG * GROUP), F32),
            pltpu.VMEM((ways, tokens, H * HD // ways), BF),
        ],
    )


def _owner(net, me, place, other):
    slot = jnp.bitwise_xor(me[0], place) if net.S == 4 else place
    return slot * 2 + (1 - me[1] if other else me[1])


def out_kernel(net, me, out_rows, *refs):
    heads, parts = refs[: 2 * net.S], refs[2 * net.S :]
    tokens, size = heads[0].shape
    weight = out_rows[pl.ds(pl.multiple_of(me[1] * size, size), size), :]
    for side in (1, 0):
        for first in range(side * net.S, (side + 1) * net.S, 2):
            rows = jnp.concatenate([heads[first][...], heads[first + 1][...]], axis=0)
            got = jnp.dot(rows, weight, preferred_element_type=F32).astype(BF)
            for k in range(2):
                parts[first + k][...] = got[k * tokens : (k + 1) * tokens, :]


def out_forward(net, me, heads, out_rows):
    tokens = heads[0].shape[0]
    return _call(
        functools.partial(out_kernel, net),
        "out_forward",
        [_shape(tokens, out_rows.shape[1])] * (2 * net.S),
        [me, out_rows, *heads],
    )


def _blocks(net, n):
    piece = n // (net.S * net.Z)
    return piece, [s * net.Z + z for z in range(net.Z) for s in range(net.S)]


def middle_kernel(net, x, gains, left, left_last, right, right_last, mid_out, h2_out):
    half = left.shape[0]
    for rows, one, two in ((slice(0, half), left, left_last), (slice(half, 2 * half), right, right_last)):
        mid = x[rows, :].astype(F32) + (one[...].astype(F32) + two[...].astype(F32))
        mid_out[rows, :] = mid
        h2 = (mid * _mean_scale(mid) * gains[1:2, :]).astype(BF)
        piece, places = _blocks(net, mid.shape[1])
        for k, place in enumerate(places):
            h2_out[rows, k * piece : (k + 1) * piece] = h2[:, place * piece : (place + 1) * piece]


def middle_forward(net, x, gains, parts):
    return _call(
        functools.partial(middle_kernel, net),
        "middle_forward",
        (_shape(*x.shape, dtype=F32), _shape(*x.shape)),
        [x, gains, *parts],
    )


def middle_back_kernel(net, mid_ref, gains, cot, left, left_last, right, right_last, grad_out, low_out, gain_out):
    half = left.shape[0]
    total = jnp.zeros((1, mid_ref.shape[1]), F32)
    gain = gains[1:2, :]
    for rows, one, two in ((slice(0, half), left, left_last), (slice(half, 2 * half), right, right_last)):
        came = one[...].astype(F32) + two[...].astype(F32)
        piece, places = _blocks(net, came.shape[1])
        back = [None] * len(places)
        for k, place in enumerate(places):
            back[place] = came[:, k * piece : (k + 1) * piece]
        upstream = jnp.concatenate(back, axis=1)
        mid = mid_ref[rows, :]
        scale = _mean_scale(mid)
        scaled = gain * upstream
        total = total + jnp.sum(upstream * mid * scale, axis=0, keepdims=True)
        inner = jnp.mean(scaled * mid, axis=1, keepdims=True)
        grad = cot[rows, :].astype(F32) + scale * scaled - mid * (scale * scale * scale * inner)
        grad_out[rows, :] = grad
        low_out[rows, :] = grad.astype(BF)
    gain_out[...] = jnp.broadcast_to(total, gain_out.shape)


def middle_back(net, mid, gains, cot, parts):
    return _call(
        functools.partial(middle_back_kernel, net),
        "middle_back",
        (_shape(*mid.shape, dtype=F32), _shape(*mid.shape), _shape(8, mid.shape[1], dtype=F32)),
        [mid, gains, cot, *parts],
    )


def _tiles(rows, size):
    tiles, held, left = [], [], size
    for k, n in enumerate(rows):
        first = 0
        while first < n:
            take = min(left, n - first)
            held.append((k, first, take))
            first, left = first + take, left - take
            if not left:
                tiles.append(held)
                held, left = [], size
    assert not held
    return tiles


def hidden_back_kernel(net, count, me, down_rows, *refs):
    rows_in, (all_out, grad_out) = refs[:count], refs[count:]
    wide = grad_out.shape[1]
    weight = down_rows[pl.ds(pl.multiple_of(me[1] * wide, 16), wide), :]
    at = 0
    for ref in rows_in:
        all_out[at : at + ref.shape[0], :] = ref[...]
        at += ref.shape[0]
    step = at // 4
    for first in range(0, at, step):
        rows = slice(first, first + step)
        grad_out[rows, :] = _nt(all_out[rows, :], weight)


def hidden_back(net, me, d, down_rows):
    rows = sum(a.shape[0] for a in d)
    return _call(
        functools.partial(hidden_back_kernel, net, len(d)),
        "hidden_back",
        (
            _shape(rows, down_rows.shape[1]),
            _shape(rows, down_rows.shape[0] // 2, dtype=F32),
        ),
        [me, down_rows, *d],
    )


def _send(copies, source, target, sem):
    copy = pltpu.make_async_copy(source, target, sem)
    copy.start()
    copies.append(copy)


def ffn_forward_kernel(tiles, *refs):
    count = len({k for tile in tiles for k, _, _ in tile})
    h, gu_w = refs[:count], refs[count]
    h_out, hid_out, slope_out, hv, gv, hidv, slopev, sem_in, sem_out = refs[count + 1 :]
    wide = hid_out.shape[1]
    size = hv.shape[1]
    gu_copy = pltpu.make_async_copy(gu_w, gv, sem_in.at[len(tiles), 0])
    copies = []
    for t, tile in enumerate(tiles):
        at = 0
        copies.append([])
        for n, (k, first, rows) in enumerate(tile):
            _send(
                copies[t], h[k].at[pl.ds(first, rows)], hv.at[t, pl.ds(at, rows)], sem_in.at[t, n]
            )
            at += rows
        if t == 0:
            gu_copy.start()
    sent = []
    for t in range(len(tiles)):
        rows = pl.ds(t * size, size)
        for c in copies[t] + ([gu_copy] if t == 0 else []):
            c.wait()
        _send(sent, hv.at[t], h_out.at[rows], sem_out.at[t, 0])
        both = jnp.dot(hv[t], gv[...], preferred_element_type=F32)
        gate = both[:, :wide]
        up = both[:, wide:]
        sigma = jax.nn.sigmoid(gate)
        silu = gate * sigma
        hidv[t] = (silu * up).astype(BF)
        _send(sent, hidv.at[t], hid_out.at[rows], sem_out.at[t, 1])
        slopev[t] = jnp.concatenate(
            [up * sigma * (1.0 + gate * (1.0 - sigma)), silu], axis=1
        ).astype(BF)
        _send(sent, slopev.at[t], slope_out.at[rows], sem_out.at[t, 2])
    for copy in sent:
        copy.wait()


def ffn_forward(h, gu_w, tokens):
    width = gu_w.shape[0]
    wide = gu_w.shape[1] // 2
    size = 2 * tokens
    tiles = _tiles([a.shape[0] for a in h], size)
    steps = len(tiles)
    return _call(
        functools.partial(ffn_forward_kernel, tiles),
        "ffn_forward",
        [_shape(steps * size, n) for n in (width, wide, 2 * wide)],
        [*h, gu_w],
        [
            pltpu.VMEM((steps, size, width), BF),
            pltpu.VMEM((width, 2 * wide), BF),
            pltpu.VMEM((steps, size, wide), BF),
            pltpu.VMEM((steps, size, 2 * wide), BF),
            pltpu.SemaphoreType.DMA((steps + 1, 5)),
            pltpu.SemaphoreType.DMA((steps, 3)),
        ],
        memory=pl.ANY,
    )


def down_grad_kernel(net, me, hidden, rows, mine, sent, grad):
    wide = hidden.shape[1]
    step = 512
    for first in range(0, rows.shape[1], step):
        grad[:, first : first + step] = _tn(hidden[...], rows[:, first : first + step]).astype(BF)
    r = wide // net.Z
    for k in range(net.Z // 2):
        low = grad[2 * k * r : (2 * k + 1) * r, :]
        high = grad[(2 * k + 1) * r : (2 * k + 2) * r, :]
        here = slice(k * r, (k + 1) * r)
        mine[here, :] = jnp.where(me[1] == 0, low, high)
        sent[here, :] = jnp.where(me[1] == 0, high, low)


def down_grad(net, me, hidden, rows):
    half = _shape(hidden.shape[1] // 2, rows.shape[1])
    return _call(
        functools.partial(down_grad_kernel, net),
        "down_grad",
        (half, half),
        [me, hidden, rows],
        [pltpu.VMEM((hidden.shape[1], rows.shape[1]), BF)],
    )


def gu_grad_kernel(rows, grad, out):
    out[...] = _tn(rows[...], grad[...]).astype(BF)


def gu_weight_grad(rows, grad):
    count, width = rows.shape
    wide = grad.shape[1]
    size = 512
    return pl.pallas_call(
        gu_grad_kernel,
        grid=(width // size,),
        out_shape=_shape(width, wide),
        in_specs=[
            pl.BlockSpec((count, size), lambda i: (0, i)),
            pl.BlockSpec((count, wide), lambda i: (0, 0)),
        ],
        out_specs=pl.BlockSpec((size, wide), lambda i: (i, 0)),
        compiler_params=pltpu.CompilerParams(vmem_limit_bytes=VMEM_BYTES),
        cost_estimate=pl.CostEstimate(flops=1, bytes_accessed=1, transcendentals=0),
        name="gu_weight_grad",
    )(rows, grad)


def ffn_back_kernel(splits, grad, slope, gu_w, *refs):
    results = len({k for tile in splits for k, _, _ in tile})
    outs = refs[:results]
    dgu_out, gradv, slopev, gv, dguv, xv, sem_in, sem_out = refs[results:]
    size, wide = gradv.shape[1:]
    gu_copy = pltpu.make_async_copy(gu_w, gv, sem_in.at[len(splits), 0])
    copies = []
    for t in range(len(splits)):
        rows = pl.ds(t * size, size)
        copies.append([])
        _send(copies[t], grad.at[rows], gradv.at[t], sem_in.at[t, 0])
        _send(copies[t], slope.at[rows], slopev.at[t], sem_in.at[t, 1])
        if t == 0:
            gu_copy.start()
    sent = []
    for t, split in enumerate(splits):
        for c in copies[t]:
            c.wait()
        up = gradv[t]
        dguv[t] = (jnp.concatenate([up, up], axis=1) * slopev[t].astype(F32)).astype(BF)
        _send(sent, dguv.at[t], dgu_out.at[pl.ds(t * size, size)], sem_out.at[t, 0])
        if t == 0:
            gu_copy.wait()
        xv[t] = _nt(dguv[t], gv[...]).astype(BF)
        at = 0
        for n, (k, first, take) in enumerate(split):
            _send(sent, xv.at[t, pl.ds(at, take)], outs[k].at[pl.ds(first, take)], sem_out.at[t, 1 + n])
            at += take
    for copy in sent:
        copy.wait()


def ffn_back(net, grad, slope, gu_w, tokens):
    width = gu_w.shape[0]
    rows, wide = grad.shape
    size = 2 * tokens
    splits = _tiles([tokens] * (2 * net.S), size)
    steps = len(splits)
    return _call(
        functools.partial(ffn_back_kernel, splits),
        "ffn_back",
        [_shape(tokens, width)] * (2 * net.S) + [_shape(rows, 2 * wide)],
        [grad, slope, gu_w],
        [
            pltpu.VMEM((steps, size, wide), F32),
            pltpu.VMEM((steps, size, 2 * wide), BF),
            pltpu.VMEM((width, 2 * wide), BF),
            pltpu.VMEM((steps, size, 2 * wide), BF),
            pltpu.VMEM((steps, size, width), BF),
            pltpu.SemaphoreType.DMA((steps + 1, 2)),
            pltpu.SemaphoreType.DMA((steps, 6)),
        ],
        memory=pl.ANY,
    )


def out_back_kernel(net, count, me, out_rows, *refs):
    rows_in, parts = refs[:count], refs[count:]
    tokens, size = parts[0].shape
    weight = out_rows[pl.ds(pl.multiple_of(me[1] * size, size), size), :]
    group = count // 2
    for side in range(2):
        rows = jnp.concatenate([ref[...] for ref in rows_in[side * group : (side + 1) * group]], axis=0)
        got = _nt(rows, weight).astype(BF)
        for place in range(net.S):
            part = parts[(1 - side) * net.S + place]
            part[...] = got[place * tokens : (place + 1) * tokens, :]


def out_back(net, me, out_rows, rows, tokens):
    return _call(
        functools.partial(out_back_kernel, net, len(rows)),
        "out_back",
        [_shape(tokens, out_rows.shape[0] // 2)] * (2 * net.S),
        [me, out_rows, *rows],
    )


def out_grad_kernel(net, count, *refs):
    heads, rows_in, grad_out = refs[: 2 * net.S], refs[2 * net.S : -1], refs[-1]
    group = count // 2
    total = None
    for side in range(2):
        left = jnp.concatenate(
            [ref[...] for ref in heads[(1 - side) * net.S : (2 - side) * net.S]], axis=0
        )
        right = jnp.concatenate([ref[...] for ref in rows_in[side * group : (side + 1) * group]], axis=0)
        part = _tn(left, right)
        total = part if total is None else total + part
    grad_out[...] = total.astype(BF)


def out_weight_grad(net, heads, rows):
    return _call(
        functools.partial(out_grad_kernel, net, len(rows)),
        "out_weight_grad",
        _shape(heads[0].shape[1], rows[0].shape[1]),
        [*heads, *rows],
    )


def back_kernel(net, table, order, here, me, q_in, att, lse, cos, sin, kv, *refs):
    parts = refs[: 2 * net.S]
    dq_out, dkv_same, dkv_other, sorted_kv, dk, dv, grad = refs[2 * net.S :]
    for number, part in enumerate(parts):
        grad[_owner(net, me, number % net.S, number >= net.S)] = part[...]
    _sort_keys(order, kv, sorted_kv)
    dk[...] = jnp.zeros_like(dk)
    dv[...] = jnp.zeros_like(dv)
    scale = 1.0 / math.sqrt(HD)
    half = HD // 2
    per_chunk = grad.shape[2] // HD
    for blk in range(2):
        rows = slice(blk * GROUP, (blk + 1) * GROUP)
        group = here[blk]
        lo, hi = _span(group, table)
        cosine, sine = cos[rows, :], sin[rows, :]
        for hg in range(H // HG):
            width = HG * GROUP
            q = _stack(q_in, rows, hg * HG, HG)
            da = jnp.concatenate(
                [
                    grad[
                        head // per_chunk,
                        rows,
                        (head % per_chunk) * HD : (head % per_chunk + 1) * HD,
                    ]
                    for head in range(hg * HG, (hg + 1) * HG)
                ],
                axis=0,
            )
            kept = _stack(att, rows, hg * HG, HG)
            delta = jnp.sum(da.astype(F32) * kept, axis=1, keepdims=True)
            delta = jnp.transpose(jnp.broadcast_to(delta, (width, 128)))[:1, :]
            shift = lse[blk, hg : hg + 1, :]
            pos = group * GROUP + lax.rem(
                lax.broadcasted_iota(jnp.int32, (1, width), 1), GROUP
            )
            start = _starts(pos, table)

            def step(t, dq):
                at = pl.ds(pl.multiple_of(t * TILE, TILE), TILE)
                k = sorted_kv[at, :HD]
                s = _nt(k, q)
                key = t * TILE + lax.broadcasted_iota(jnp.int32, (TILE, width), 0)
                p = jnp.where((key >= start) & (key <= pos), jnp.exp(s - shift), 0.0)
                dp = _nt(sorted_kv[at, HD:], da)
                ds = (p * (dp - delta)).astype(BF)
                dv[at, :] += jnp.dot(p.astype(BF), da, preferred_element_type=F32)
                dk[at, :] += jnp.dot(ds, q, preferred_element_type=F32)
                return dq + _tn(k, ds)

            dq = jnp.transpose(lax.fori_loop(lo, hi, step, jnp.zeros((HD, width), F32)))
            dq = dq * scale
            for h in range(HG):
                head = hg * HG + h
                a = dq[h * GROUP : (h + 1) * GROUP, :half]
                b = dq[h * GROUP : (h + 1) * GROUP, half:]
                dq_out[rows, head * HD : head * HD + half] = (a * cosine + b * sine).astype(BF)
                dq_out[rows, head * HD + half : (head + 1) * HD] = (
                    b * cosine - a * sine
                ).astype(BF)
    for side, rows, at in _key_blocks(net, me, order):
        target = (dkv_same, dkv_other)[side]
        target[rows, :HD] = dk[at, :].astype(BF)
        target[rows, HD:] = dv[at, :].astype(BF)


def attend_back(net, table, order, here, me, q, grads, att, lse, cos, sin, kv):
    slot_rows = kv.shape[0]
    half = _shape(slot_rows // 2, 2 * HD)
    return _call(
        functools.partial(back_kernel, net),
        "attend_back",
        (_shape(*q.shape), half, half),
        [table, order, here, me, q, att, lse, cos, sin, kv, *grads],
        [
            pltpu.VMEM((slot_rows, 2 * HD), BF),
            pltpu.VMEM((slot_rows, HD), F32),
            pltpu.VMEM((slot_rows, HD), F32),
            pltpu.VMEM((len(grads), *grads[0].shape), BF),
        ],
    )


def up_back_kernel(net, count, results, me, dq, cqn, low_ref, gain_ref, *refs):
    pieces, outs = refs[:count], refs[count : count + results]
    low_grad_out, up_q, grad = refs[count + results :]
    _join(net, me, pieces, up_q)
    wide = dq.shape[1]
    gain = gain_ref[...]
    upstream = _nt(dq[...], up_q[...])
    low = low_ref[...]
    scale = _mean_scale(low)
    gain_grad = jnp.sum(upstream * low * scale, axis=0, keepdims=True)
    scaled = gain * upstream
    inner = jnp.mean(scaled * low, axis=1, keepdims=True)
    low_grad_out[...] = (scale * scaled - low * (scale * scale * scale * inner)).astype(BF)
    step = 1024
    for first in range(0, wide, step):
        grad[:, first : first + step] = _tn(cqn[...], dq[:, first : first + step]).astype(BF)
    grad[:, wide:] = jnp.transpose(
        jnp.broadcast_to(gain_grad, (128, gain_grad.shape[1]))
    ).astype(BF)
    _part(net, me, grad, outs)


def up_back(net, me, dq, cqn, low, gain, pieces):
    tokens, low_rank = low.shape
    wide = H * HD + 128
    outs = _out_pieces(net, low_rank, wide)
    *parts, grad = _call(
        functools.partial(up_back_kernel, net, len(pieces), len(outs)),
        "up_back",
        outs + [_shape(tokens, low_rank)],
        [me, dq, cqn, low, gain, *pieces],
        [pltpu.VMEM((low_rank, H * HD), BF), pltpu.VMEM((low_rank, wide), BF)],
    )
    return parts, grad


def _out_pieces(net, rows, wide):
    if not net.whole_pieces(rows):
        return [_shape(rows // (2 * net.S), wide)] * (2 * net.S)
    return [_shape(rows, wide)]


def project_back_kernel(net, count, results, me, x_ref, low_grad, both, cos, sin, mid_grad, gains, mid_gain, *refs):
    pieces, outs = refs[:count], refs[count : count + results]
    in_out, whole, grad = refs[count + results :]
    _join(net, me, pieces, whole)
    width = whole.shape[0]
    low_rank = low_grad.shape[1]
    last = low_rank + 2 * HD
    half = HD // 2
    a, b = both[:, :half].astype(F32), both[:, half:HD].astype(F32)
    upstream_parts = jnp.concatenate(
        [
            low_grad[...],
            (a * cos[...] + b * sin[...]).astype(BF),
            (b * cos[...] - a * sin[...]).astype(BF),
            both[:, HD:].astype(BF),
        ],
        axis=1,
    )
    x = x_ref[...].astype(F32)
    scale = _mean_scale(x)
    gain = gains[:1, :]
    normed = (x * scale * gain).astype(BF)
    for first in range(0, last, 512):
        grad[:, first : first + 512] = _tn(normed, upstream_parts[:, first : first + 512]).astype(BF)
    upstream = _nt(upstream_parts, whole[:, :last])
    gain_grad = jnp.sum(upstream * x * scale, axis=0, keepdims=True)
    scaled = gain * upstream
    inner = jnp.mean(scaled * x, axis=1, keepdims=True)
    in_out[...] = (mid_grad[...] + scale * scaled - x * (scale * scale * scale * inner)).astype(BF)
    tall = lax.broadcasted_iota(jnp.int32, (128, width), 0)
    both_gains = jnp.where(
        tall == 0, jnp.broadcast_to(gain_grad, (128, width)),
        jnp.broadcast_to(mid_gain[:1, :], (128, width)),
    )
    grad[:, last:] = jnp.transpose(both_gains).astype(BF)
    _part(net, me, grad, outs)


def project_back(net, me, x, low_grad, both, cos, sin, mid_grad, gains, mid_gain, pieces):
    tokens, width = x.shape
    wide = pieces[0].shape[1]
    outs = _out_pieces(net, width, wide)
    *parts, in_grad = _call(
        functools.partial(project_back_kernel, net, len(pieces), len(outs)),
        "project_back",
        outs + [_shape(tokens, width)],
        [me, x, low_grad, both, cos, sin, mid_grad, gains, mid_gain, *pieces],
        [pltpu.VMEM((width, wide), BF), pltpu.VMEM((width, wide), BF)],
    )
    return parts, in_grad


def finish_kernel(got, low_out, key_out, value_out, gains_out):
    low_rank = low_out.shape[1]
    low_out[...] = got[:, :low_rank].astype(F32)
    key_out[...] = got[:, low_rank : low_rank + HD].astype(F32)
    value_out[...] = got[:, low_rank + HD : low_rank + 2 * HD].astype(F32)
    gains_out[...] = jnp.transpose(got[:, low_rank + 2 * HD :].astype(F32))[: gains_out.shape[0], :]


def finish(got, low_rank):
    rows = got.shape[0]
    return _call(
        finish_kernel,
        "finish",
        (
            _shape(rows, low_rank, dtype=F32),
            _shape(rows, HD, dtype=F32),
            _shape(rows, HD, dtype=F32),
            _shape(8, rows, dtype=F32),
        ),
        [got],
    )


def share_kernel(net, me, hidden, down_rows, *parts):
    tokens = parts[0].shape[0]
    wide = hidden.shape[1]
    weight = down_rows[pl.ds(pl.multiple_of(me[1] * wide, 16), wide), :]
    for first in range(0, len(parts), 2):
        rows = hidden[first * tokens : (first + 2) * tokens, :]
        got = jnp.dot(rows, weight, preferred_element_type=F32).astype(BF)
        for k in range(2):
            parts[first + k][...] = got[k * tokens : (k + 1) * tokens, :]


def down_share(net, me, hidden, down_rows, tokens):
    return _call(
        functools.partial(share_kernel, net),
        "down_share",
        [_shape(tokens, down_rows.shape[1])] * (2 * net.S),
        [me, hidden, down_rows],
    )


def body(
    net,
    hidden_in, seq_lens, group_order, attn_gain, wq_down, q_gain, wq_up, w_key, w_value, w_out,
    ffn_gain, w_gate, w_up, w_down, out_grad,
):
    lengths = seq_lens[0]
    order = group_order[0]
    tokens = hidden_in.shape[0]
    low_rank = wq_up.shape[0] * net.S * net.Z * 2
    last = low_rank + 2 * HD
    me = net.me()
    place = lax.axis_index("z") * 2 + lax.axis_index("c")
    rows_here = place * tokens + jnp.arange(tokens, dtype=jnp.int32)
    seq_pos, valid = place_info(rows_here, order, lengths, tokens)
    cosine, sine = rope_tables(seq_pos, HD)
    table = jnp.concatenate([jnp.cumsum(lengths), lengths]).astype(jnp.int32)
    here = lax.dynamic_slice_in_dim(order, 2 * place, 2, 0)
    kept = {}

    rows = wq_down.shape[0]
    q_column = jnp.pad(column(q_gain), ((0, rows - q_gain.shape[0]), (0, 0)))
    gains = (
        column(attn_gain)
        + jnp.roll(column(ffn_gain), 1, axis=1)
        + jnp.roll(q_column, 2, axis=1)
    )
    up_z = net.z_gather(wq_up)
    out_rows = net.rows_gather(w_out)
    down_rows = net.rows_gather(w_down)
    gu_mine = net.cols_exchange(w_gate, w_up)
    first_z = net.z_gather(jnp.concatenate([wq_down, w_key, w_value, gains], axis=1))
    first_z, gu_mine = tie(first_z, gu_mine)

    def first_two(*moved):
        *moved, kept["up_z"] = tie(*moved, up_z)
        return moved

    first_pieces = net.weight_pieces(net.spread(first_z, (None, first_two)))
    query_low, kv, gains = project(net, me, hidden_in, cosine, sine, first_pieces, low_rank)
    kv, out_rows = tie(kv, out_rows)
    both = net.rows_gather(kv)

    def up_two(*moved):
        *moved, kept["both"] = tie(*moved, both)
        return moved

    up_z = kept["up_z"]
    up_pieces = net.weight_pieces(net.spread(up_z, (None, up_two)))
    both = kept["both"]
    gain_q = gains[2:3].reshape(-1, rows)[:, : q_gain.shape[0]].reshape(1, low_rank)
    cot = (out_grad.astype(F32) * valid[:, None].astype(F32)).astype(BF)
    cot, *_ = tie(cot, *up_pieces)

    def cot_one(*moved):
        kept["attend"] = attend(
            net, table, order, here, me, query_low, gain_q, cosine, sine, both, up_pieces
        )
        count = len(moved)
        *kept["attend"], a, b = tie(*kept["attend"], *moved, *moved[: 2 - count])
        return [a, b][:count]

    def cot_two(*moved):
        heads = net.exchange_pieces(kept["attend"][: 2 * net.S])
        parts = out_forward(net, me, heads, out_rows)
        kept["heads"] = heads
        done = tie(*moved, *parts)
        kept["out_parts"] = done[len(moved) :]
        return done[: len(moved)]

    cot_same = net.spread(cot, (cot_one, cot_two))
    cot_other = net.swap_all(cot_same)
    gu_chunk = net.z_gather(gu_mine)
    query_normed, query_rows, attended, log_total = kept["attend"][2 * net.S :]
    heads = kept["heads"]
    out_parts = kept["out_parts"]
    middle, normed_two = middle_forward(
        net, hidden_in, gains, net.collect(out_parts[: net.S], out_parts[net.S :])
    )

    two_same = net.spread(normed_two)
    two_all = [*net.swap_all(two_same), *two_same]
    cot_rows, hidden_grad = hidden_back(net, me, [*cot_other, *cot_same], down_rows)
    gu_chunk, hidden_grad, cot_rows, *two_all = tie(gu_chunk, hidden_grad, cot_rows, *two_all)
    two_rows, hidden, slopes = ffn_forward(two_all, gu_chunk, tokens)
    *back_parts, gu_grad = ffn_back(net, hidden_grad, slopes, gu_chunk, tokens)

    def back_one(*came):
        *_, kept["hidden"], kept["gu_grad"] = tie(*came, hidden, gu_grad)
        kept["grad_down"] = net.rows_return(*down_grad(net, me, kept["hidden"], cot_rows))
        return came

    def back_two(*moved):
        *moved, _ = tie(*moved, kept["grad_down"])
        gu_grad, *_ = tie(kept["gu_grad"], *moved)
        kept["grad_gu"] = lax.dot_general(
            two_rows, gu_grad, (((0,), (0,)), ((), ())), preferred_element_type=F32
        ).astype(BF)
        return moved

    def back_three(*moved):
        down = net.z_scatter(kept["grad_down"])
        *moved, kept["grad_gu"], kept["down"] = tie(*moved, kept["grad_gu"], down)
        return moved

    middle_grad, middle_low, middle_gain = middle_back(
        net,
        middle,
        gains,
        cot,
        net.collect(
            back_parts[net.S :], back_parts[: net.S], (back_one, back_two, back_three)
        ),
    )
    grad_gu = net.z_scatter(kept["grad_gu"])

    def middle_one(*moved):
        hidden, *_ = tie(kept["hidden"], middle_low)
        shares = down_share(net, me, hidden, down_rows, tokens)
        done = tie(*moved, *shares)
        kept["shares"] = done[len(moved) :]
        return done[: len(moved)]

    middle_same = net.spread(middle_low, (middle_one,))
    middle_all = [*net.swap_all(middle_same), *middle_same]
    heads_grad = net.exchange_pieces(out_back(net, me, out_rows, middle_all, tokens))
    grad_out = net.rows_return(*net.rows_parted(out_weight_grad(net, heads, middle_all)))
    count = 2 * net.S
    done = tie(*heads_grad, *kept["shares"], grad_out)
    heads_grad, shares, grad_out = done[:count], done[count:-1], done[-1]

    def result_two(*moved):
        backs = attend_back(
            net, table, order, here, me, query_rows, heads_grad, attended, log_total, cosine,
            sine, both,
        )
        *moved, kept["query_pre"], same, other, kept["grad_gu"] = tie(*moved, *backs, grad_gu)
        kept["both_grads"] = same.astype(F32) + net.swap_c(other).astype(F32)
        return moved

    upper, upper_last, lower, lower_last = net.collect(
        shares[net.S :], shares[: net.S], (None, result_two)
    )
    layer_out = (
        middle
        + jnp.concatenate(
            [upper + upper_last.astype(F32), lower + lower_last.astype(F32)], axis=0
        )
    ).astype(BF)
    both_sum = net.z_scatter(kept["both_grads"])
    up_parts, low_grad = up_back(
        net, me, kept["query_pre"], query_normed, query_low, gain_q, up_pieces
    )

    grad_out = net.z_scatter(grad_out)
    grad_down = kept["down"].astype(F32)

    def whole(parts):
        upper, upper_last, lower, lower_last = parts
        return net.z_scatter(
            jnp.concatenate(
                [upper + upper_last.astype(F32), lower + lower_last.astype(F32)], axis=0
            )
        )

    both_sum, *up_parts = tie(both_sum, *up_parts)
    def up_one(*came):
        *came, kept["both_sum"] = tie(*came, both_sum)
        return came

    def up_two(*moved):
        first_parts, kept["in_grad"] = project_back(
            net, me, hidden_in, low_grad, kept["both_sum"], cosine, sine, middle_grad, gains,
            middle_gain, first_pieces,
        )
        done = tie(*moved, *first_parts)
        kept["first_parts"] = done[len(moved) :]
        return done[: len(moved)]

    up_out = whole(net.collect(*net.weight_sides(up_parts), (up_one, up_two)))

    def first_two(*moved):
        *moved, kept["grad_out"], kept["grad_gu"] = tie(*moved, grad_out, kept["grad_gu"])
        return moved

    first_out = whole(
        net.collect(*net.weight_sides(kept["first_parts"]), (None, first_two))
    )
    grad_out = kept["grad_out"].astype(F32)
    grad_gate, grad_upward = net.cols_return(kept["grad_gu"])
    grad_low, grad_key, grad_value, grad_gains = finish(first_out, low_rank)
    return (
        layer_out,
        kept["in_grad"],
        grad_gains[0],
        grad_low,
        up_out[:, H * HD].astype(F32),
        up_out[:, : H * HD].astype(F32),
        grad_key,
        grad_value,
        grad_out,
        grad_gains[1],
        grad_gate,
        grad_upward,
        grad_down,
    )


def solution(mesh):
    slots, seq = mesh.devices.shape
    fine = Mesh(mesh.devices.reshape(slots, seq // 2, 2), ("slot", "z", "c"))
    every = ("slot", "z", "c")
    matrix = P(every, None)
    vector = P(every)
    net = Net(slots, seq // 2)
    return jax.shard_map(
        functools.partial(body, net),
        mesh=fine,
        in_specs=(
            matrix, P("slot", None), P("slot", None), vector, matrix, vector, matrix, matrix,
            matrix, matrix, vector, matrix, matrix, matrix, matrix,
        ),
        out_specs=(
            matrix, matrix, vector, matrix, vector, matrix, matrix, matrix, matrix, vector,
            matrix, matrix, matrix,
        ),
        check_vma=False,
    )
```

```python
import functools
import math

import jax
import jax.numpy as jnp
from jax import lax
from jax.experimental import pallas as pl
from jax.experimental.pallas import tpu as pltpu
from jax.sharding import Mesh
from jax.sharding import PartitionSpec as P

H = 16
HD = 256
GROUP = 96
TILE = 256
HG = 8
VMEM_BYTES = 60 << 20

EPS = 1e-05
ROPE_BASE = 10000.0
BF = jnp.bfloat16
F32 = jnp.float32


class Net:
    def __init__(self, slots, depth):
        self.S = slots
        self.Z = depth

    def me(self):
        return jnp.stack([lax.axis_index("slot"), lax.axis_index("c")]).astype(jnp.int32)

    def whole_pieces(self, rows):
        return self.S != 4

    def segments(self, n):
        if self.S != 4:
            return [(0, 0, n)]
        half = n // 2
        return [(0, 0, n), (1, 0, n), (2, 0, n), (3, 0, half), (3, half, n - half)]

    def swap_c(self, a):
        return lax.ppermute(a, "c", [(0, 1), (1, 0)])

    def swap_x(self, a):
        return lax.ppermute(a, "slot", [(0, 1), (1, 0), (2, 3), (3, 2)])

    def swap_y(self, a):
        return lax.ppermute(a, "slot", [(0, 2), (2, 0), (1, 3), (3, 1)])

    def spread(self, a, during=()):
        first, second = [*during, None, None][:2]
        if self.S != 4:
            a = lax.all_gather(a, "slot", axis=0, tiled=True)
            for step in (first, second):
                if step is not None:
                    (a,) = step(a)
            return [a]
        half = a.shape[0] // 2
        ax = self.swap_x(a)
        ay = self.swap_y(a)
        if first is not None:
            ax, ay = first(ax, ay)
        d0 = self.swap_y(ax[:half])
        d1 = self.swap_x(ay[half:])
        if second is not None:
            d0, d1 = second(d0, d1)
        return [a, ax, ay, d0, d1]

    def swap_all(self, pieces):
        return [self.swap_c(a) for a in pieces]

    def weight_pieces(self, same):
        other = self.swap_all(same)
        if self.S == 4:
            return [*same, *other]
        n = same[0].shape[1]
        r = same[0].shape[0] // (self.S * self.Z)
        first = lax.axis_index("c") == 0
        same = same[0].reshape(self.S, self.Z, 1, r, n)
        other = other[0].reshape(self.S, self.Z, 1, r, n)
        pair = [jnp.where(first, same, other), jnp.where(first, other, same)]
        return [jnp.concatenate(pair, axis=2).reshape(-1, n)]

    def weight_sides(self, parts):
        if self.S == 4:
            return parts[:4], parts[4:]
        n = parts[0].shape[1]
        whole = parts[0].reshape(self.S, self.Z, 2, -1, n)
        r = whole.shape[3]
        core = lax.axis_index("c")
        return tuple(
            [
                lax.dynamic_slice_in_dim(whole[slot], k, 1, 1).reshape(self.Z * r, n)
                for slot in range(self.S)
            ]
            for k in (core, 1 - core)
        )

    def collect(self, same, other, during=()):
        first, second, third = [*during, None, None, None][:3]
        came = self.swap_all(other)
        if first is not None:
            came = first(*came)
        held = [a.astype(F32) + b.astype(F32) for a, b in zip(same, came)]
        half = same[0].shape[0] // 2
        if self.S != 4:
            total = jnp.concatenate(held, axis=0).astype(BF)
            for step in (second, third):
                if step is not None:
                    (total,) = step(total)
            total = lax.psum_scatter(total, "slot", scatter_dimension=0, tiled=True)
            upper, lower = total[:half].astype(F32), total[half:].astype(F32)
            return [upper, jnp.zeros_like(total[:half]), lower, jnp.zeros_like(total[half:])]
        via_x = self.swap_x(jnp.concatenate([held[1][:half], held[3][:half]], axis=0).astype(BF))
        via_y = self.swap_y(jnp.concatenate([held[2][half:], held[3][half:]], axis=0).astype(BF))
        if second is not None:
            via_x, via_y = second(via_x, via_y)
        via_x, via_y = via_x.astype(F32), via_y.astype(F32)
        upper = held[0][:half] + via_x[:half]
        lower = held[0][half:] + via_y[: via_y.shape[0] // 2]
        upper_last = self.swap_y((held[2][:half] + via_x[half:]).astype(BF))
        lower_last = self.swap_x((held[1][half:] + via_y[via_y.shape[0] // 2 :]).astype(BF))
        if third is not None:
            upper_last, lower_last = third(upper_last, lower_last)
        return [upper, upper_last, lower, lower_last]

    def z_gather(self, w):
        return lax.all_gather(w, "z", axis=0, tiled=True)

    def z_scatter(self, g):
        return lax.psum_scatter(g.astype(BF), "z", scatter_dimension=0, tiled=True)

    def rows_gather(self, w):
        return lax.all_gather(w, ("z", "c"), axis=0, tiled=True)

    def rows_return(self, mine, sent):
        return rows_joined(self.me(), mine, self.swap_c(sent))

    def cols_exchange(self, gate, up):
        r, n = gate.shape
        ways = 2 * self.S
        parts = jnp.concatenate(
            [gate.reshape(r, ways, n // ways), up.reshape(r, ways, n // ways)], axis=2
        ).transpose(1, 0, 2)
        return self.exchange(parts).reshape(ways * r, 2 * n // ways)

    def cols_return(self, mine):
        ways = 2 * self.S
        m = mine.shape[1] // 2
        parts = self.exchange(mine.reshape(ways, -1, 2 * m)).transpose(1, 0, 2)
        r = parts.shape[0]
        return (
            parts[:, :, :m].reshape(r, ways * m).astype(F32),
            parts[:, :, m:].reshape(r, ways * m).astype(F32),
        )

    def exchange(self, a):
        return lax.all_to_all(a, ("slot", "c"), 0, 0, tiled=True)

    def exchange_pieces(self, pieces):
        if self.S == 4:
            ways = 2 * self.S
            moved = [pieces[0]]
            for number in range(1, ways):
                step = 2 * (number % self.S) + number // self.S
                moved.append(
                    lax.ppermute(pieces[number], ("slot", "c"), [(i, i ^ step) for i in range(ways)])
                )
            return moved
        first = lax.axis_index("c") == 0
        same, other = jnp.stack(pieces[: self.S]), jnp.stack(pieces[self.S :])
        pair = jnp.stack([jnp.where(first, same, other), jnp.where(first, other, same)], axis=1)
        pair = self.exchange(pair.reshape(2 * self.S, *pieces[0].shape))
        low, high = pair[0::2], pair[1::2]
        return [*jnp.where(first, low, high), *jnp.where(first, high, low)]


def tie(*arrays):
    return lax.optimization_barrier(arrays)


def column(a):
    return jnp.pad(a.reshape(-1, 1), ((0, 0), (0, 127)))


def place_info(row_index, order, lengths, tokens):
    device = row_index // tokens
    local = row_index % tokens
    pick = 2 * device + local // GROUP
    table = jnp.arange(order.shape[0], dtype=jnp.int32)
    group_id = jnp.sum(jnp.where(pick[:, None] == table[None, :], order[None, :], 0), axis=1)
    slot_pos = group_id * GROUP + local % GROUP
    ends = jnp.cumsum(lengths)
    passed = slot_pos[:, None] >= ends[None, :]
    segment = jnp.sum(passed.astype(jnp.int32), axis=1)
    start = jnp.sum(jnp.where(passed, lengths[None, :], 0), axis=1)
    return (slot_pos - start, segment < lengths.shape[0])


def rope_tables(position, width):
    half = width // 2
    freq = ROPE_BASE ** (-2.0 * jnp.arange(half, dtype=F32) / width)
    angle = position.astype(F32)[:, None] * freq[None, :]
    return (jnp.cos(angle), jnp.sin(angle))


def _call(kernel, name, out_shape, args, scratch=(), memory=None, flops=1):
    specs = [
        pl.BlockSpec(
            memory_space=pltpu.SMEM
            if a.dtype == jnp.int32 and a.ndim == 1
            else (memory or pltpu.VMEM)
        )
        for a in args
    ]
    many = isinstance(out_shape, (tuple, list))
    out_specs = [pl.BlockSpec(memory_space=memory or pltpu.VMEM)] * (len(out_shape) if many else 1)
    return pl.pallas_call(
        kernel,
        out_shape=out_shape,
        in_specs=specs,
        out_specs=out_specs if many else out_specs[0],
        scratch_shapes=list(scratch),
        compiler_params=pltpu.CompilerParams(vmem_limit_bytes=VMEM_BYTES),
        cost_estimate=pl.CostEstimate(flops=flops, bytes_accessed=1, transcendentals=0),
        name=name,
    )(*args)


def _shape(*dims, dtype=BF):
    return jax.ShapeDtypeStruct(dims, dtype)


def _nt(a, b):
    return lax.dot_general(a, b, (((1,), (1,)), ((), ())), preferred_element_type=F32)


def _tn(a, b):
    return lax.dot_general(a, b, (((0,), (0,)), ((), ())), preferred_element_type=F32)


def _row_place(net, me, place, z, other, r):
    slot = jnp.bitwise_xor(me[0], place) if net.S == 4 else place
    core = 1 - me[1] if other else me[1]
    return pl.multiple_of(((slot * net.Z + z) * 2 + core) * r, r)


def _join(net, me, pieces, whole):
    if len(pieces) == 1:
        whole[...] = pieces[0][...]
        return
    r = whole.shape[0] // (net.S * net.Z * 2)
    for side in range(2):
        for (place, first, count), ref in zip(net.segments(net.Z * r), pieces[side * 5 : side * 5 + 5]):
            for k in range(count // r):
                at = _row_place(net, me, place, first // r + k, side == 1, r)
                whole[pl.ds(at, r), :] = ref[k * r : (k + 1) * r, :]


def _part(net, me, whole, pieces):
    if len(pieces) == 1:
        pieces[0][...] = whole[...]
        return
    r = whole.shape[0] // (net.S * net.Z * 2)
    for side in range(2):
        for place in range(net.S):
            for z in range(net.Z):
                at = _row_place(net, me, place, z, side == 1, r)
                pieces[side * net.S + place][z * r : (z + 1) * r, :] = whole[pl.ds(at, r), :]


def _mean_scale(values):
    return lax.rsqrt(jnp.mean(values * values, axis=1, keepdims=True) + EPS)


def project_kernel(net, count, me, x_ref, cos, sin, *refs):
    pieces, (low_out, kv_out, gain_out, whole) = refs[:count], refs[count:]
    _join(net, me, pieces, whole)
    width = whole.shape[0]
    low_rank = low_out.shape[1]
    last = low_rank + 2 * HD
    gains = jnp.transpose(whole[:, last:].astype(F32))
    gain_out[...] = gains[: gain_out.shape[0], :]
    x = x_ref[...].astype(F32)
    normed = (x * _mean_scale(x) * gains[:1, :]).astype(BF)
    low_out[...] = jnp.dot(normed, whole[:, :low_rank], preferred_element_type=F32)
    both = jnp.dot(normed, whole[:, low_rank:last], preferred_element_type=F32)
    half = HD // 2
    a, b = both[:, :half], both[:, half:HD]
    kv_out[:, :half] = (a * cos[...] - b * sin[...]).astype(BF)
    kv_out[:, half:HD] = (a * sin[...] + b * cos[...]).astype(BF)
    kv_out[:, HD:] = both[:, HD:].astype(BF)


def project(net, me, x, cos, sin, pieces, low_rank):
    tokens, width = x.shape
    wide = pieces[0].shape[1]
    return _call(
        functools.partial(project_kernel, net, len(pieces)),
        "project",
        (_shape(tokens, low_rank, dtype=F32), _shape(tokens, 2 * HD), _shape(8, width, dtype=F32)),
        [me, x, cos, sin, *pieces],
        [pltpu.VMEM((width, wide), BF)],
    )


def _starts(pos, table):
    start = jnp.zeros_like(pos)
    count = table.shape[0] // 2
    for k in range(count):
        start = start + jnp.where(pos >= table[k], table[count + k], 0)
    return start


def _start_of(pos, table):
    start = jnp.int32(0)
    count = table.shape[0] // 2
    for k in range(count):
        start = start + jnp.where(pos >= table[k], table[count + k], 0)
    return start


def _span(group, table):
    return _start_of(group * GROUP, table) // TILE, (group * GROUP + GROUP - 1) // TILE + 1


def _stack(ref, rows, first, heads):
    return jnp.concatenate(
        [ref[rows, (first + h) * HD : (first + h + 1) * HD] for h in range(heads)], axis=0
    )


def _sort_keys(order, kv, sorted_kv):
    for b in range(kv.shape[0] // GROUP):
        at = pl.ds(pl.multiple_of(order[b] * GROUP, GROUP), GROUP)
        sorted_kv[at, :] = kv[b * GROUP : (b + 1) * GROUP, :]


def _key_blocks(net, me, order):
    for side in range(2):
        core = me[1] if side == 0 else 1 - me[1]
        for k in range(2 * net.Z):
            group = order[2 * (2 * (k // 2) + core) + k % 2]
            at = pl.ds(pl.multiple_of(group * GROUP, GROUP), GROUP)
            yield side, slice(k * GROUP, (k + 1) * GROUP), at


def attend_kernel(net, count, table, order, here, me, low, gain, cos, sin, kv, *refs):
    pieces, parts = refs[:count], refs[count : count + 2 * net.S]
    cqn_out, q_out, att_out, lse_out, up_q, sorted_kv, scores, chunk_out = refs[
        count + 2 * net.S :
    ]
    _join(net, me, pieces, up_q)
    _sort_keys(order, kv, sorted_kv)
    cqn_out[...] = (low[...] * _mean_scale(low[...]) * gain[...]).astype(BF)
    scale = 1.0 / math.sqrt(HD)
    half = HD // 2
    per_chunk = chunk_out.shape[2] // HD
    for h in range(H):
        full = jnp.dot(
            cqn_out[...], up_q[:, h * HD : (h + 1) * HD], preferred_element_type=F32
        )
        a, b = full[:, :half], full[:, half:]
        q_out[:, h * HD : h * HD + half] = ((a * cos[...] - b * sin[...]) * scale).astype(BF)
        q_out[:, h * HD + half : (h + 1) * HD] = (
            (a * sin[...] + b * cos[...]) * scale
        ).astype(BF)
    for blk in range(2):
        rows = slice(blk * GROUP, (blk + 1) * GROUP)
        group = here[blk]
        lo, hi = _span(group, table)
        for hg in range(H // HG):
            q = _stack(q_out, rows, hg * HG, HG)
            width = HG * GROUP
            pos = group * GROUP + lax.rem(
                lax.broadcasted_iota(jnp.int32, (1, width), 1), GROUP
            )
            start = _starts(pos, table)

            def score(t, top):
                at = pl.ds(pl.multiple_of(t * TILE, TILE), TILE)
                s = _nt(sorted_kv[at, :HD], q)
                key = t * TILE + lax.broadcasted_iota(jnp.int32, (TILE, width), 0)
                s = jnp.where((key >= start) & (key <= pos), s, -1e30)
                scores[at, :] = s
                return jnp.maximum(top, jnp.max(s, axis=0, keepdims=True))

            top = lax.fori_loop(lo, hi, score, jnp.full((1, width), -1e30, F32))

            def weigh(t, carry):
                total, summed = carry
                at = pl.ds(pl.multiple_of(t * TILE, TILE), TILE)
                p = jnp.exp(scores[at, :] - top)
                total = total + jnp.sum(p, axis=0, keepdims=True)
                return total, summed + _tn(sorted_kv[at, HD:], p.astype(BF))

            total, summed = lax.fori_loop(
                lo, hi, weigh, (jnp.zeros((1, width), F32), jnp.zeros((HD, width), F32))
            )
            lse_out[blk, hg : hg + 1, :] = top + jnp.log(total)
            att = jnp.transpose(summed / total)
            for h in range(HG):
                head = hg * HG + h
                piece = att[h * GROUP : (h + 1) * GROUP, :]
                att_out[rows, head * HD : (head + 1) * HD] = piece
                lanes = slice((head % per_chunk) * HD, (head % per_chunk + 1) * HD)
                chunk_out[head // per_chunk, rows, lanes] = piece.astype(BF)
    for number, part in enumerate(parts):
        part[...] = chunk_out[_owner(net, me, number % net.S, number >= net.S)]


def attend(net, table, order, here, me, low, gain, cos, sin, kv, pieces):
    tokens, low_rank = low.shape
    slot_rows = kv.shape[0]
    ways = 2 * net.S
    return _call(
        functools.partial(attend_kernel, net, len(pieces)),
        "attend",
        [_shape(tokens, H * HD // ways)] * ways
        + [
            _shape(tokens, low_rank),
            _shape(tokens, H * HD),
            _shape(tokens, H * HD, dtype=F32),
            _shape(2, H // HG, HG * GROUP, dtype=F32),
        ],
        [table, order, here, me, low, gain, cos, sin, kv, *pieces],
        [
            pltpu.VMEM((low_rank, H * HD), BF),
            pltpu.VMEM((slot_rows, 2 * HD), BF),
            pltpu.VMEM((slot_rows, HG * GROUP), F32),
            pltpu.VMEM((ways, tokens, H * HD // ways), BF),
        ],
    )


def _owner(net, me, place, other):
    slot = jnp.bitwise_xor(me[0], place) if net.S == 4 else place
    return slot * 2 + (1 - me[1] if other else me[1])


def out_kernel(net, me, out_rows, *refs):
    heads, parts = refs[: 2 * net.S], refs[2 * net.S :]
    tokens, size = heads[0].shape
    weight = out_rows[pl.ds(pl.multiple_of(me[1] * size, size), size), :]
    for side in (1, 0):
        for first in range(side * net.S, (side + 1) * net.S, 2):
            rows = jnp.concatenate([heads[first][...], heads[first + 1][...]], axis=0)
            got = jnp.dot(rows, weight, preferred_element_type=F32).astype(BF)
            for k in range(2):
                parts[first + k][...] = got[k * tokens : (k + 1) * tokens, :]


def out_forward(net, me, heads, out_rows):
    tokens = heads[0].shape[0]
    return _call(
        functools.partial(out_kernel, net),
        "out_forward",
        [_shape(tokens, out_rows.shape[1])] * (2 * net.S),
        [me, out_rows, *heads],
    )


def _blocks(net, n):
    piece = n // (net.S * net.Z)
    return piece, [s * net.Z + z for z in range(net.Z) for s in range(net.S)]


def middle_kernel(net, x, gains, left, left_last, right, right_last, mid_out, h2_out):
    half = left.shape[0]
    for rows, one, two in ((slice(0, half), left, left_last), (slice(half, 2 * half), right, right_last)):
        mid = x[rows, :].astype(F32) + (one[...].astype(F32) + two[...].astype(F32))
        mid_out[rows, :] = mid
        h2 = (mid * _mean_scale(mid) * gains[1:2, :]).astype(BF)
        piece, places = _blocks(net, mid.shape[1])
        for k, place in enumerate(places):
            h2_out[rows, k * piece : (k + 1) * piece] = h2[:, place * piece : (place + 1) * piece]


def middle_forward(net, x, gains, parts):
    return _call(
        functools.partial(middle_kernel, net),
        "middle_forward",
        (_shape(*x.shape, dtype=F32), _shape(*x.shape)),
        [x, gains, *parts],
    )


def middle_back_kernel(net, mid_ref, gains, cot, left, left_last, right, right_last, grad_out, low_out, gain_out):
    half = left.shape[0]
    total = jnp.zeros((1, mid_ref.shape[1]), F32)
    gain = gains[1:2, :]
    for rows, one, two in ((slice(0, half), left, left_last), (slice(half, 2 * half), right, right_last)):
        came = one[...].astype(F32) + two[...].astype(F32)
        piece, places = _blocks(net, came.shape[1])
        back = [None] * len(places)
        for k, place in enumerate(places):
            back[place] = came[:, k * piece : (k + 1) * piece]
        upstream = jnp.concatenate(back, axis=1)
        mid = mid_ref[rows, :]
        scale = _mean_scale(mid)
        scaled = gain * upstream
        total = total + jnp.sum(upstream * mid * scale, axis=0, keepdims=True)
        inner = jnp.mean(scaled * mid, axis=1, keepdims=True)
        grad = cot[rows, :].astype(F32) + scale * scaled - mid * (scale * scale * scale * inner)
        grad_out[rows, :] = grad
        low_out[rows, :] = grad.astype(BF)
    gain_out[...] = jnp.broadcast_to(total, gain_out.shape)


def middle_back(net, mid, gains, cot, parts):
    return _call(
        functools.partial(middle_back_kernel, net),
        "middle_back",
        (_shape(*mid.shape, dtype=F32), _shape(*mid.shape), _shape(8, mid.shape[1], dtype=F32)),
        [mid, gains, cot, *parts],
    )


def _tiles(rows, size):
    tiles, held, left = [], [], size
    for k, n in enumerate(rows):
        first = 0
        while first < n:
            take = min(left, n - first)
            held.append((k, first, take))
            first, left = first + take, left - take
            if not left:
                tiles.append(held)
                held, left = [], size
    assert not held
    return tiles


def hidden_back_kernel(net, count, me, down_rows, *refs):
    rows_in, (all_out, grad_out) = refs[:count], refs[count:]
    wide = grad_out.shape[1]
    weight = down_rows[pl.ds(pl.multiple_of(me[1] * wide, 16), wide), :]
    at = 0
    for ref in rows_in:
        all_out[at : at + ref.shape[0], :] = ref[...]
        at += ref.shape[0]
    step = at // 4
    for first in range(0, at, step):
        rows = slice(first, first + step)
        grad_out[rows, :] = _nt(all_out[rows, :], weight)


def hidden_back(net, me, d, down_rows):
    rows = sum(a.shape[0] for a in d)
    return _call(
        functools.partial(hidden_back_kernel, net, len(d)),
        "hidden_back",
        (
            _shape(rows, down_rows.shape[1]),
            _shape(rows, down_rows.shape[0] // 2, dtype=F32),
        ),
        [me, down_rows, *d],
    )


def _send(copies, source, target, sem):
    copy = pltpu.make_async_copy(source, target, sem)
    copy.start()
    copies.append(copy)


def ffn_forward_kernel(tiles, *refs):
    count = len({k for tile in tiles for k, _, _ in tile})
    h, gu_w = refs[:count], refs[count]
    h_out, hid_out, slope_out, hv, gv, hidv, slopev, sem_in, sem_out = refs[count + 1 :]
    wide = hid_out.shape[1]
    size = hv.shape[1]
    gu_copy = pltpu.make_async_copy(gu_w, gv, sem_in.at[len(tiles), 0])
    copies = []
    for t, tile in enumerate(tiles):
        at = 0
        copies.append([])
        for n, (k, first, rows) in enumerate(tile):
            _send(
                copies[t], h[k].at[pl.ds(first, rows)], hv.at[t, pl.ds(at, rows)], sem_in.at[t, n]
            )
            at += rows
        if t == 0:
            gu_copy.start()
    sent = []
    for t in range(len(tiles)):
        rows = pl.ds(t * size, size)
        for c in copies[t] + ([gu_copy] if t == 0 else []):
            c.wait()
        _send(sent, hv.at[t], h_out.at[rows], sem_out.at[t, 0])
        both = jnp.dot(hv[t], gv[...], preferred_element_type=F32)
        gate = both[:, :wide]
        up = both[:, wide:]
        sigma = jax.nn.sigmoid(gate)
        silu = gate * sigma
        hidv[t] = (silu * up).astype(BF)
        _send(sent, hidv.at[t], hid_out.at[rows], sem_out.at[t, 1])
        slopev[t] = jnp.concatenate(
            [up * sigma * (1.0 + gate * (1.0 - sigma)), silu], axis=1
        ).astype(BF)
        _send(sent, slopev.at[t], slope_out.at[rows], sem_out.at[t, 2])
    for copy in sent:
        copy.wait()


def ffn_forward(h, gu_w, tokens):
    width = gu_w.shape[0]
    wide = gu_w.shape[1] // 2
    size = 2 * tokens
    tiles = _tiles([a.shape[0] for a in h], size)
    steps = len(tiles)
    return _call(
        functools.partial(ffn_forward_kernel, tiles),
        "ffn_forward",
        [_shape(steps * size, n) for n in (width, wide, 2 * wide)],
        [*h, gu_w],
        [
            pltpu.VMEM((steps, size, width), BF),
            pltpu.VMEM((width, 2 * wide), BF),
            pltpu.VMEM((steps, size, wide), BF),
            pltpu.VMEM((steps, size, 2 * wide), BF),
            pltpu.SemaphoreType.DMA((steps + 1, 5)),
            pltpu.SemaphoreType.DMA((steps, 3)),
        ],
        memory=pl.ANY,
    )


def down_grad_kernel(net, me, hidden, rows, mine, sent, grad):
    wide = hidden.shape[1]
    step = 512
    for first in range(0, rows.shape[1], step):
        grad[:, first : first + step] = _tn(hidden[...], rows[:, first : first + step]).astype(BF)
    _part_rows(net, me, grad, mine, sent)


def down_grad(net, me, hidden, rows):
    half = _shape(hidden.shape[1] // 2, rows.shape[1])
    return _call(
        functools.partial(down_grad_kernel, net),
        "down_grad",
        (half, half),
        [me, hidden, rows],
        [pltpu.VMEM((hidden.shape[1], rows.shape[1]), BF)],
    )


def gu_grad_kernel(rows, grad, out):
    out[...] = _tn(rows[...], grad[...]).astype(BF)


def gu_weight_grad(rows, grad):
    count, width = rows.shape
    wide = grad.shape[1]
    size = 512
    return pl.pallas_call(
        gu_grad_kernel,
        grid=(width // size,),
        out_shape=_shape(width, wide),
        in_specs=[
            pl.BlockSpec((count, size), lambda i: (0, i)),
            pl.BlockSpec((count, wide), lambda i: (0, 0)),
        ],
        out_specs=pl.BlockSpec((size, wide), lambda i: (i, 0)),
        compiler_params=pltpu.CompilerParams(vmem_limit_bytes=VMEM_BYTES),
        cost_estimate=pl.CostEstimate(flops=1, bytes_accessed=1, transcendentals=0),
        name="gu_weight_grad",
    )(rows, grad)


def ffn_back_kernel(splits, grad, slope, gu_w, *refs):
    results = len({k for tile in splits for k, _, _ in tile})
    outs = refs[:results]
    dgu_out, gradv, slopev, gv, dguv, xv, sem_in, sem_out = refs[results:]
    size, wide = gradv.shape[1:]
    gu_copy = pltpu.make_async_copy(gu_w, gv, sem_in.at[len(splits), 0])
    copies = []
    for t in range(len(splits)):
        rows = pl.ds(t * size, size)
        copies.append([])
        _send(copies[t], grad.at[rows], gradv.at[t], sem_in.at[t, 0])
        _send(copies[t], slope.at[rows], slopev.at[t], sem_in.at[t, 1])
        if t == 0:
            gu_copy.start()
    sent = []
    for t, split in enumerate(splits):
        for c in copies[t]:
            c.wait()
        up = gradv[t]
        dguv[t] = (jnp.concatenate([up, up], axis=1) * slopev[t].astype(F32)).astype(BF)
        _send(sent, dguv.at[t], dgu_out.at[pl.ds(t * size, size)], sem_out.at[t, 0])
        if t == 0:
            gu_copy.wait()
        xv[t] = _nt(dguv[t], gv[...]).astype(BF)
        at = 0
        for n, (k, first, take) in enumerate(split):
            _send(sent, xv.at[t, pl.ds(at, take)], outs[k].at[pl.ds(first, take)], sem_out.at[t, 1 + n])
            at += take
    for copy in sent:
        copy.wait()


def ffn_back(net, grad, slope, gu_w, tokens):
    width = gu_w.shape[0]
    rows, wide = grad.shape
    size = 2 * tokens
    splits = _tiles([tokens] * (2 * net.S), size)
    steps = len(splits)
    return _call(
        functools.partial(ffn_back_kernel, splits),
        "ffn_back",
        [_shape(tokens, width)] * (2 * net.S) + [_shape(rows, 2 * wide)],
        [grad, slope, gu_w],
        [
            pltpu.VMEM((steps, size, wide), F32),
            pltpu.VMEM((steps, size, 2 * wide), BF),
            pltpu.VMEM((width, 2 * wide), BF),
            pltpu.VMEM((steps, size, 2 * wide), BF),
            pltpu.VMEM((steps, size, width), BF),
            pltpu.SemaphoreType.DMA((steps + 1, 2)),
            pltpu.SemaphoreType.DMA((steps, 6)),
        ],
        memory=pl.ANY,
    )


def out_back_kernel(net, count, me, out_rows, *refs):
    rows_in, parts = refs[:count], refs[count:]
    tokens, size = parts[0].shape
    weight = out_rows[pl.ds(pl.multiple_of(me[1] * size, size), size), :]
    group = count // 2
    for side in range(2):
        rows = jnp.concatenate([ref[...] for ref in rows_in[side * group : (side + 1) * group]], axis=0)
        got = _nt(rows, weight).astype(BF)
        for place in range(net.S):
            part = parts[(1 - side) * net.S + place]
            part[...] = got[place * tokens : (place + 1) * tokens, :]


def out_back(net, me, out_rows, rows, tokens):
    return _call(
        functools.partial(out_back_kernel, net, len(rows)),
        "out_back",
        [_shape(tokens, out_rows.shape[0] // 2)] * (2 * net.S),
        [me, out_rows, *rows],
    )


def _part_rows(net, me, grad, mine, sent):
    r = grad.shape[0] // net.Z
    for k in range(net.Z // 2):
        low = grad[2 * k * r : (2 * k + 1) * r, :]
        high = grad[(2 * k + 1) * r : (2 * k + 2) * r, :]
        here = slice(k * r, (k + 1) * r)
        mine[here, :] = jnp.where(me[1] == 0, low, high)
        sent[here, :] = jnp.where(me[1] == 0, high, low)


def rows_joined_kernel(me, mine, came, out):
    half = mine.shape[0]
    out[pl.ds(pl.multiple_of(me[1] * half, half), half), :] = mine[...]
    out[pl.ds(pl.multiple_of((1 - me[1]) * half, half), half), :] = came[...]


def rows_joined(me, mine, came):
    half, width = mine.shape
    return _call(rows_joined_kernel, "rows_joined", _shape(2 * half, width), [me, mine, came])


def out_grad_kernel(net, count, me, *refs):
    heads, rows_in = refs[: 2 * net.S], refs[2 * net.S : -3]
    mine, sent, grad = refs[-3:]
    group = count // 2
    total = None
    for side in range(2):
        left = jnp.concatenate(
            [ref[...] for ref in heads[(1 - side) * net.S : (2 - side) * net.S]], axis=0
        )
        right = jnp.concatenate([ref[...] for ref in rows_in[side * group : (side + 1) * group]], axis=0)
        part = _tn(left, right)
        total = part if total is None else total + part
    grad[...] = total.astype(BF)
    _part_rows(net, me, grad, mine, sent)


def out_weight_grad(net, me, heads, rows):
    size, width = heads[0].shape[1], rows[0].shape[1]
    return _call(
        functools.partial(out_grad_kernel, net, len(rows)),
        "out_weight_grad",
        (_shape(size // 2, width), _shape(size // 2, width)),
        [me, *heads, *rows],
        [pltpu.VMEM((size, width), BF)],
        flops=8 * heads[0].size * len(heads) * rows[0].shape[1],
    )


def back_kernel(net, table, order, here, me, q_in, att, lse, cos, sin, kv, *refs):
    parts = refs[: 2 * net.S]
    dq_out, dkv_same, dkv_other, sorted_kv, dk, dv, grad = refs[2 * net.S :]
    for number, part in enumerate(parts):
        grad[_owner(net, me, number % net.S, number >= net.S)] = part[...]
    _sort_keys(order, kv, sorted_kv)
    dk[...] = jnp.zeros_like(dk)
    dv[...] = jnp.zeros_like(dv)
    scale = 1.0 / math.sqrt(HD)
    half = HD // 2
    per_chunk = grad.shape[2] // HD
    for blk in range(2):
        rows = slice(blk * GROUP, (blk + 1) * GROUP)
        group = here[blk]
        lo, hi = _span(group, table)
        cosine, sine = cos[rows, :], sin[rows, :]
        for hg in range(H // HG):
            width = HG * GROUP
            q = _stack(q_in, rows, hg * HG, HG)
            da = jnp.concatenate(
                [
                    grad[
                        head // per_chunk,
                        rows,
                        (head % per_chunk) * HD : (head % per_chunk + 1) * HD,
                    ]
                    for head in range(hg * HG, (hg + 1) * HG)
                ],
                axis=0,
            )
            kept = _stack(att, rows, hg * HG, HG)
            delta = jnp.sum(da.astype(F32) * kept, axis=1, keepdims=True)
            delta = jnp.transpose(jnp.broadcast_to(delta, (width, 128)))[:1, :]
            shift = lse[blk, hg : hg + 1, :]
            pos = group * GROUP + lax.rem(
                lax.broadcasted_iota(jnp.int32, (1, width), 1), GROUP
            )
            start = _starts(pos, table)

            def step(t, dq):
                at = pl.ds(pl.multiple_of(t * TILE, TILE), TILE)
                k = sorted_kv[at, :HD]
                s = _nt(k, q)
                key = t * TILE + lax.broadcasted_iota(jnp.int32, (TILE, width), 0)
                p = jnp.where((key >= start) & (key <= pos), jnp.exp(s - shift), 0.0)
                dp = _nt(sorted_kv[at, HD:], da)
                ds = (p * (dp - delta)).astype(BF)
                dv[at, :] += jnp.dot(p.astype(BF), da, preferred_element_type=F32)
                dk[at, :] += jnp.dot(ds, q, preferred_element_type=F32)
                return dq + _tn(k, ds)

            dq = jnp.transpose(lax.fori_loop(lo, hi, step, jnp.zeros((HD, width), F32)))
            dq = dq * scale
            for h in range(HG):
                head = hg * HG + h
                a = dq[h * GROUP : (h + 1) * GROUP, :half]
                b = dq[h * GROUP : (h + 1) * GROUP, half:]
                dq_out[rows, head * HD : head * HD + half] = (a * cosine + b * sine).astype(BF)
                dq_out[rows, head * HD + half : (head + 1) * HD] = (
                    b * cosine - a * sine
                ).astype(BF)
    for side, rows, at in _key_blocks(net, me, order):
        target = (dkv_same, dkv_other)[side]
        target[rows, :HD] = dk[at, :].astype(BF)
        target[rows, HD:] = dv[at, :].astype(BF)


def attend_back(net, table, order, here, me, q, grads, att, lse, cos, sin, kv):
    slot_rows = kv.shape[0]
    half = _shape(slot_rows // 2, 2 * HD)
    return _call(
        functools.partial(back_kernel, net),
        "attend_back",
        (_shape(*q.shape), half, half),
        [table, order, here, me, q, att, lse, cos, sin, kv, *grads],
        [
            pltpu.VMEM((slot_rows, 2 * HD), BF),
            pltpu.VMEM((slot_rows, HD), F32),
            pltpu.VMEM((slot_rows, HD), F32),
            pltpu.VMEM((len(grads), *grads[0].shape), BF),
        ],
    )


def up_grad_kernel(net, me, dq, cqn, *refs):
    outs, grad = refs[:-1], refs[-1]
    step = 1024
    for first in range(0, dq.shape[1], step):
        grad[:, first : first + step] = _tn(cqn[...], dq[:, first : first + step]).astype(BF)
    _part(net, me, grad, outs)


def up_weight_grad(net, me, dq, cqn):
    low_rank, wide = cqn.shape[1], dq.shape[1]
    return _call(
        functools.partial(up_grad_kernel, net),
        "up_weight_grad",
        _out_pieces(net, low_rank, wide),
        [me, dq, cqn],
        [pltpu.VMEM((low_rank, wide), BF)],
    )


def up_back_kernel(net, me, dq, low_ref, gain_ref, *refs):
    pieces, (low_grad_out, gain_out, up_q) = refs[:-3], refs[-3:]
    _join(net, me, pieces, up_q)
    gain = gain_ref[...]
    upstream = _nt(dq[...], up_q[...])
    low = low_ref[...]
    scale = _mean_scale(low)
    gain_grad = jnp.sum(upstream * low * scale, axis=0, keepdims=True)
    gain_out[...] = jnp.broadcast_to(gain_grad, gain_out.shape)
    scaled = gain * upstream
    inner = jnp.mean(scaled * low, axis=1, keepdims=True)
    low_grad_out[...] = (scale * scaled - low * (scale * scale * scale * inner)).astype(BF)


def up_back(net, dq, low, gain, pieces, me):
    tokens, low_rank = low.shape
    return _call(
        functools.partial(up_back_kernel, net),
        "up_back",
        [_shape(tokens, low_rank), _shape(8, low_rank, dtype=F32)],
        [me, dq, low, gain, *pieces],
        [pltpu.VMEM((low_rank, dq.shape[1]), BF)],
    )


def _out_pieces(net, rows, wide):
    if not net.whole_pieces(rows):
        return [_shape(rows // (2 * net.S), wide)] * (2 * net.S)
    return [_shape(rows, wide)]


def project_back_kernel(net, count, results, me, x_ref, low_grad, both, cos, sin, mid_grad, gains, mid_gain, q_gain_grad, *refs):
    pieces, outs = refs[:count], refs[count : count + results]
    in_out, whole, grad = refs[count + results :]
    _join(net, me, pieces, whole)
    width = whole.shape[0]
    low_rank = low_grad.shape[1]
    last = low_rank + 2 * HD
    half = HD // 2
    a, b = both[:, :half].astype(F32), both[:, half:HD].astype(F32)
    upstream_parts = jnp.concatenate(
        [
            low_grad[...],
            (a * cos[...] + b * sin[...]).astype(BF),
            (b * cos[...] - a * sin[...]).astype(BF),
            both[:, HD:].astype(BF),
        ],
        axis=1,
    )
    x = x_ref[...].astype(F32)
    scale = _mean_scale(x)
    gain = gains[:1, :]
    normed = (x * scale * gain).astype(BF)
    for first in range(0, last, 512):
        grad[:, first : first + 512] = _tn(normed, upstream_parts[:, first : first + 512]).astype(BF)
    upstream = _nt(upstream_parts, whole[:, :last])
    gain_grad = jnp.sum(upstream * x * scale, axis=0, keepdims=True)
    scaled = gain * upstream
    inner = jnp.mean(scaled * x, axis=1, keepdims=True)
    in_out[...] = (mid_grad[...] + scale * scaled - x * (scale * scale * scale * inner)).astype(BF)
    tall = lax.broadcasted_iota(jnp.int32, (128, width), 0)
    both_gains = jnp.where(
        tall == 0,
        jnp.broadcast_to(gain_grad, (128, width)),
        jnp.where(
            tall == 1,
            jnp.broadcast_to(mid_gain[:1, :], (128, width)),
            jnp.broadcast_to(q_gain_grad[...], (128, width)),
        ),
    )
    grad[:, last:] = jnp.transpose(both_gains).astype(BF)
    _part(net, me, grad, outs)


def project_back(
    net, me, x, low_grad, both, cos, sin, mid_grad, gains, mid_gain, q_gain_grad, pieces
):
    tokens, width = x.shape
    wide = pieces[0].shape[1]
    outs = _out_pieces(net, width, wide)
    *parts, in_grad = _call(
        functools.partial(project_back_kernel, net, len(pieces), len(outs)),
        "project_back",
        outs + [_shape(tokens, width)],
        [me, x, low_grad, both, cos, sin, mid_grad, gains, mid_gain, q_gain_grad, *pieces],
        [pltpu.VMEM((width, wide), BF), pltpu.VMEM((width, wide), BF)],
    )
    return parts, in_grad


def finish_kernel(got, low_out, key_out, value_out, gains_out):
    low_rank = low_out.shape[1]
    low_out[...] = got[:, :low_rank].astype(F32)
    key_out[...] = got[:, low_rank : low_rank + HD].astype(F32)
    value_out[...] = got[:, low_rank + HD : low_rank + 2 * HD].astype(F32)
    gains_out[...] = jnp.transpose(got[:, low_rank + 2 * HD :].astype(F32))[: gains_out.shape[0], :]


def finish(got, low_rank):
    rows = got.shape[0]
    return _call(
        finish_kernel,
        "finish",
        (
            _shape(rows, low_rank, dtype=F32),
            _shape(rows, HD, dtype=F32),
            _shape(rows, HD, dtype=F32),
            _shape(8, rows, dtype=F32),
        ),
        [got],
    )


def share_kernel(net, me, hidden, down_rows, *parts):
    tokens = parts[0].shape[0]
    wide = hidden.shape[1]
    weight = down_rows[pl.ds(pl.multiple_of(me[1] * wide, 16), wide), :]
    for first in range(0, len(parts), 2):
        rows = hidden[first * tokens : (first + 2) * tokens, :]
        got = jnp.dot(rows, weight, preferred_element_type=F32).astype(BF)
        for k in range(2):
            parts[first + k][...] = got[k * tokens : (k + 1) * tokens, :]


def down_share(net, me, hidden, down_rows, tokens):
    return _call(
        functools.partial(share_kernel, net),
        "down_share",
        [_shape(tokens, down_rows.shape[1])] * (2 * net.S),
        [me, hidden, down_rows],
    )


def body(
    net,
    hidden_in, seq_lens, group_order, attn_gain, wq_down, q_gain, wq_up, w_key, w_value, w_out,
    ffn_gain, w_gate, w_up, w_down, out_grad,
):
    lengths = seq_lens[0]
    order = group_order[0]
    tokens = hidden_in.shape[0]
    low_rank = wq_up.shape[0] * net.S * net.Z * 2
    last = low_rank + 2 * HD
    me = net.me()
    place = lax.axis_index("z") * 2 + lax.axis_index("c")
    rows_here = place * tokens + jnp.arange(tokens, dtype=jnp.int32)
    seq_pos, valid = place_info(rows_here, order, lengths, tokens)
    cosine, sine = rope_tables(seq_pos, HD)
    table = jnp.concatenate([jnp.cumsum(lengths), lengths]).astype(jnp.int32)
    here = lax.dynamic_slice_in_dim(order, 2 * place, 2, 0)
    kept = {}

    rows = wq_down.shape[0]
    q_column = jnp.pad(column(q_gain), ((0, rows - q_gain.shape[0]), (0, 0)))
    gains = (
        column(attn_gain)
        + jnp.roll(column(ffn_gain), 1, axis=1)
        + jnp.roll(q_column, 2, axis=1)
    )
    up_z = net.z_gather(wq_up)
    out_rows = net.rows_gather(w_out)
    down_rows = net.rows_gather(w_down)
    gu_mine = net.cols_exchange(w_gate, w_up)
    first_z = net.z_gather(jnp.concatenate([wq_down, w_key, w_value, gains], axis=1))
    first_z, gu_mine = tie(first_z, gu_mine)

    def first_two(*moved):
        *moved, kept["up_z"] = tie(*moved, up_z)
        return moved

    first_pieces = net.weight_pieces(net.spread(first_z, (None, first_two)))
    query_low, kv, gains = project(net, me, hidden_in, cosine, sine, first_pieces, low_rank)
    kv, out_rows = tie(kv, out_rows)
    both = net.rows_gather(kv)

    def up_two(*moved):
        *moved, kept["both"] = tie(*moved, both)
        return moved

    up_z = kept["up_z"]
    up_pieces = net.weight_pieces(net.spread(up_z, (None, up_two)))
    both = kept["both"]
    gain_q = gains[2:3].reshape(-1, rows)[:, : q_gain.shape[0]].reshape(1, low_rank)
    cot = (out_grad.astype(F32) * valid[:, None].astype(F32)).astype(BF)
    cot, *_ = tie(cot, *up_pieces)

    def cot_one(*moved):
        kept["attend"] = attend(
            net, table, order, here, me, query_low, gain_q, cosine, sine, both, up_pieces
        )
        count = len(moved)
        *kept["attend"], a, b = tie(*kept["attend"], *moved, *moved[: 2 - count])
        return [a, b][:count]

    def cot_two(*moved):
        heads = net.exchange_pieces(kept["attend"][: 2 * net.S])
        parts = out_forward(net, me, heads, out_rows)
        kept["heads"] = heads
        done = tie(*moved, *parts)
        kept["out_parts"] = done[len(moved) :]
        return done[: len(moved)]

    cot_same = net.spread(cot, (cot_one, cot_two))
    cot_other = net.swap_all(cot_same)
    gu_chunk = net.z_gather(gu_mine)
    query_normed, query_rows, attended, log_total = kept["attend"][2 * net.S :]
    heads = kept["heads"]
    out_parts = kept["out_parts"]
    middle, normed_two = middle_forward(
        net, hidden_in, gains, net.collect(out_parts[: net.S], out_parts[net.S :])
    )

    two_same = net.spread(normed_two)
    two_all = [*net.swap_all(two_same), *two_same]
    cot_rows, hidden_grad = hidden_back(net, me, [*cot_other, *cot_same], down_rows)
    gu_chunk, hidden_grad, cot_rows, *two_all = tie(gu_chunk, hidden_grad, cot_rows, *two_all)
    two_rows, hidden, slopes = ffn_forward(two_all, gu_chunk, tokens)
    *back_parts, gu_grad = ffn_back(net, hidden_grad, slopes, gu_chunk, tokens)

    def back_one(*came):
        *_, kept["hidden"], kept["gu_grad"] = tie(*came, hidden, gu_grad)
        kept["grad_down"] = net.rows_return(*down_grad(net, me, kept["hidden"], cot_rows))
        return came

    def back_two(*moved):
        *moved, _ = tie(*moved, kept["grad_down"])
        gu_grad, *_ = tie(kept["gu_grad"], *moved)
        kept["grad_gu"] = lax.dot_general(
            two_rows, gu_grad, (((0,), (0,)), ((), ())), preferred_element_type=F32
        ).astype(BF)
        return moved

    def back_three(*moved):
        down = net.z_scatter(kept["grad_down"])
        *moved, kept["grad_gu"], kept["down"] = tie(*moved, kept["grad_gu"], down)
        return moved

    middle_grad, middle_low, middle_gain = middle_back(
        net,
        middle,
        gains,
        cot,
        net.collect(
            back_parts[net.S :], back_parts[: net.S], (back_one, back_two, back_three)
        ),
    )
    grad_gu = net.z_scatter(kept["grad_gu"])

    def middle_one(*moved):
        hidden, *_ = tie(kept["hidden"], middle_low)
        shares = down_share(net, me, hidden, down_rows, tokens)
        done = tie(*moved, *shares)
        kept["shares"] = done[len(moved) :]
        return done[: len(moved)]

    middle_same = net.spread(middle_low, (middle_one,))
    middle_all = [*net.swap_all(middle_same), *middle_same]
    heads_grad = out_back(net, me, out_rows, middle_all, tokens)
    count = 2 * net.S
    done = tie(*heads_grad, *middle_all)
    middle_all = done[count:]
    heads_grad = net.exchange_pieces(done[:count])
    grad_mine, grad_sent = out_weight_grad(net, me, heads, middle_all)
    count = 2 * net.S
    done = tie(*heads_grad, *kept["shares"], grad_mine, grad_sent)
    heads_grad, shares = done[:count], done[count:-2]

    def result_two(*moved):
        backs = attend_back(
            net, table, order, here, me, query_rows, heads_grad, attended, log_total, cosine,
            sine, both,
        )
        *moved, kept["query_pre"], same, other = tie(*moved, *backs)
        kept["both_grads"] = same.astype(F32) + net.swap_c(other).astype(F32)
        return moved

    upper, upper_last, lower, lower_last = net.collect(
        shares[net.S :], shares[: net.S], (None, result_two)
    )
    layer_out = (
        middle
        + jnp.concatenate(
            [upper + upper_last.astype(F32), lower + lower_last.astype(F32)], axis=0
        )
    ).astype(BF)
    both_sum = net.z_scatter(kept["both_grads"])
    up_parts = up_weight_grad(net, me, kept["query_pre"], query_normed)
    *up_parts, kept["grad_gu"] = tie(*up_parts, grad_gu)
    grad_out = net.z_scatter(net.rows_return(*done[-2:]))

    def whole(parts):
        upper, upper_last, lower, lower_last = parts
        return net.z_scatter(
            jnp.concatenate(
                [upper + upper_last.astype(F32), lower + lower_last.astype(F32)], axis=0
            )
        )

    def up_one(*came):
        *came, kept["query_pre"] = tie(*came, kept["query_pre"])
        return came

    def up_two(*moved):
        low_grad, gain_grad = up_back(
            net, kept["query_pre"], query_low, gain_q, up_pieces, me
        )
        gain_grad = jnp.pad(
            gain_grad[0].reshape(-1, q_gain.shape[0]), ((0, 0), (0, rows - q_gain.shape[0]))
        ).reshape(1, -1)
        first_parts, kept["in_grad"] = project_back(
            net, me, hidden_in, low_grad, both_sum, cosine, sine, middle_grad, gains,
            middle_gain, gain_grad, first_pieces,
        )
        done = tie(*moved, *first_parts)
        kept["first_parts"] = done[len(moved) :]
        return done[: len(moved)]

    up_out = whole(net.collect(*net.weight_sides(up_parts), (up_one, up_two)))

    def first_two(*moved):
        *moved, kept["grad_out"], kept["grad_gu"], kept["down"] = tie(
            *moved, grad_out, kept["grad_gu"], kept["down"]
        )
        return moved

    first_out = whole(
        net.collect(*net.weight_sides(kept["first_parts"]), (None, first_two))
    )
    grad_out = kept["grad_out"].astype(F32)
    grad_down = kept["down"].astype(F32)
    grad_gate, grad_upward = net.cols_return(kept["grad_gu"])
    grad_low, grad_key, grad_value, grad_gains = finish(first_out, low_rank)
    return (
        layer_out,
        kept["in_grad"],
        grad_gains[0],
        grad_low,
        grad_gains[2, : q_gain.shape[0]],
        up_out.astype(F32),
        grad_key,
        grad_value,
        grad_out,
        grad_gains[1],
        grad_gate,
        grad_upward,
        grad_down,
    )


def solution(mesh):
    slots, seq = mesh.devices.shape
    fine = Mesh(mesh.devices.reshape(slots, seq // 2, 2), ("slot", "z", "c"))
    every = ("slot", "z", "c")
    matrix = P(every, None)
    vector = P(every)
    net = Net(slots, seq // 2)
    return jax.shard_map(
        functools.partial(body, net),
        mesh=fine,
        in_specs=(
            matrix, P("slot", None), P("slot", None), vector, matrix, vector, matrix, matrix,
            matrix, matrix, vector, matrix, matrix, matrix, matrix,
        ),
        out_specs=(
            matrix, matrix, vector, matrix, vector, matrix, matrix, matrix, matrix, vector,
            matrix, matrix, matrix,
        ),
        check_vma=False,
    )
```
